128 devices in a mesh: dp: 32 (over z_hi, x, y), tensor: 4 (over z_lo, core).
Axes of the slice: x: 4, y: 4, z: 4 (z_hi: 2, z_lo: 2; z = z_hi * 2 + z_lo), core: 2. Of those that a mesh axis runs over, the one named last changes fastest.
Arguments:
- tokens: bfloat16 [16384, 2048], P(('dp', 'tensor')), may hold values from -24 to 24
- lengths: int32 [32, 4], P('dp'), may hold values from 1 to 509, as said below
- attention_gain: bfloat16 [2048], P('dp'), may hold values from 0.099609375 to 1.8984375
- query_weight: bfloat16 [2048, 2048], P('dp', 'tensor'), may hold values from -0.125 to 0.125
- key_weight: bfloat16 [2048, 256], P('dp', 'tensor'), may hold values from -0.125 to 0.125
- value_weight: bfloat16 [2048, 256], P('dp', 'tensor'), may hold values from -0.125 to 0.125
- out_weight: bfloat16 [2048, 2048], P('tensor', 'dp'), may hold values from -1 to 1
- feedforward_gain: bfloat16 [2048], P('dp'), may hold values from 0.099609375 to 1.8984375
- gate_weight: bfloat16 [2048, 5632], P('dp', 'tensor'), may hold values from -0.125 to 0.125
- up_weight: bfloat16 [2048, 5632], P('dp', 'tensor'), may hold values from -0.125 to 0.125
- down_weight: bfloat16 [5632, 2048], P('tensor', 'dp'), may hold values from -0.078125 to 0.078125
- cotangent: bfloat16 [16384, 2048], P(('dp', 'tensor')), may hold values from -24 to 24
Outputs:
- output: bfloat16 [16384, 2048], P(('dp', 'tensor'))
- input_grad: bfloat16 [16384, 2048], P(('dp', 'tensor'))
- attention_gain_grad: float32 [2048], P('dp')
- query_grad: float32 [2048, 2048], P('dp', 'tensor')
- key_grad: float32 [2048, 256], P('dp', 'tensor')
- value_grad: float32 [2048, 256], P('dp', 'tensor')
- out_grad: float32 [2048, 2048], P('tensor', 'dp')
- feedforward_gain_grad: float32 [2048], P('dp')
- gate_grad: float32 [2048, 5632], P('dp', 'tensor')
- up_grad: float32 [2048, 5632], P('dp', 'tensor')
- down_grad: float32 [5632, 2048], P('tensor', 'dp')
The draws below stay inside these ranges and needn't reach their ends.
Inputs may be any that keep to these rules, and one draw needn't show every extreme that they name: Row g holds the lengths of the 4 sequences packed in order into group g; each row sums to 512.
All inputs are finite; a program needn't handle non-finite values.
Results may differ from the reference program's by a relative error of at most 0.03.
Values may be sent and summed in bfloat16 or wider, within the bound.
A program may use at most 128 MiB of HBM per device.

```python
import math
import jax
import jax.numpy as jnp
from jax import lax

D = 2048
HEADS = 32
KV_HEADS = 4
HD = 64
FF = 5632
NSEG = 4
TOK_DEV = 128
GROUP_TOK = 512
GROUPS = 32
TOKENS = 16384


def draw_lengths(key, part):
    key = jax.random.fold_in(key, 7)
    keys = jax.random.split(key, 4)
    first = jax.random.randint(keys[0], (GROUPS,), 1, TOK_DEV // 2 + 1)
    lowest = 3 * TOK_DEV + 1 - first
    highest = GROUP_TOK - 2 - first
    longest = lowest + jax.random.randint(keys[1], (GROUPS,), 0, 1 << 20) % (highest - lowest + 1)
    rest = GROUP_TOK - first - longest
    second = 1 + jax.random.randint(keys[2], (GROUPS,), 0, 1 << 20) % (rest - 1)
    third = rest - second
    chosen = jnp.arange(GROUPS) == jax.random.randint(keys[3], (), 0, GROUPS)
    first = jnp.where(chosen, 1, first)
    longest = jnp.where(chosen, GROUP_TOK - 3, longest)
    second = jnp.where(chosen, 1, second)
    third = jnp.where(chosen, 1, third)
    return jnp.stack([first, longest, second, third], axis=1).astype(jnp.int32)


def spiked(entries, own_key, source, target, parts, factor):
    owner, partner = [(jnp.arange(entries.shape[axis_at]) // (entries.shape[axis_at] // parts)).reshape([-1 if axis == axis_at else 1 for axis in range(entries.ndim)]) for axis_at in (source, target)]
    chosen = jax.random.permutation(own_key, parts)[partner]
    strong = (owner == chosen) | (owner == (partner + parts // 2) % parts)
    return jnp.where(strong, factor * entries, entries)


def block_scale(stream_key, shape, cuts, least, high):
    loudness = 1.0
    for dim, parts in cuts:
        draws = jax.random.uniform(jax.random.fold_in(jax.random.fold_in(stream_key, 6), dim), (parts,), jnp.float32, least / len(cuts), high / len(cuts))
        loudness = loudness * jnp.repeat(jnp.exp(draws), shape[dim] // parts).reshape((-1,) + (1,) * (len(shape) - 1 - dim))
    return loudness


def gaussian(own_key, extent, scale, reach, cuts=(), held_as=jnp.bfloat16):
    result = scale * jax.random.normal(own_key, extent, jnp.float32)
    if cuts:
        result = result * block_scale(own_key, extent, cuts, -0.22, 0.18)
    return jnp.clip(result, -reach, reach).astype(held_as)


def heavy_noise(rng, extent, deviation, most, cuts, heavy, kind=jnp.bfloat16):
    drawn = deviation * jax.random.normal(rng, extent, jnp.float32)
    if cuts:
        drawn = drawn * block_scale(rng, extent, cuts, -0.22, 0.18)
    return jnp.clip(spiked(drawn, jax.random.fold_in(rng, 3), *heavy), -most, most).astype(kind)


def setup_inputs(seed: int = 0) -> dict:
    seeds = jax.random.split(jax.random.key(seed), 13)
    tokens = heavy_noise(seeds[0], (TOKENS, D), 1.0, 24.0, ((0, 128),), (0, 1, 128, 5.5))
    lengths = draw_lengths(jax.random.fold_in(seeds[12], 71), 0)
    attention_gain = jnp.clip(1.0 + 0.18 * jax.random.normal(seeds[2], (D,), jnp.float32), 0.099609375, 1.8984375).astype(jnp.bfloat16)
    query_weight = gaussian(seeds[3], (D, HEADS * HD), D ** -0.5, 0.125, ((0, 32), (1, 4)))
    key_weight = gaussian(seeds[4], (D, KV_HEADS * HD), D ** -0.5, 0.125, ((0, 32), (1, 4)))
    value_weight = gaussian(seeds[5], (D, KV_HEADS * HD), D ** -0.5, 0.125, ((0, 32), (1, 4)))
    out_weight = gaussian(seeds[6], (HEADS * HD, D), (HEADS * HD // 64) ** -0.5, 1.0, ((0, 4), (1, 32)))
    feedforward_gain = jnp.clip(1.0 + 0.18 * jax.random.normal(seeds[7], (D,), jnp.float32), 0.099609375, 1.8984375).astype(jnp.bfloat16)
    gate_weight = gaussian(seeds[8], (D, FF), D ** -0.5, 0.125, ((0, 32), (1, 4)))
    up_weight = gaussian(seeds[9], (D, FF), D ** -0.5, 0.125, ((0, 32), (1, 4)))
    down_weight = gaussian(seeds[10], (FF, D), FF ** -0.5, 0.078125, ((0, 4), (1, 32)))
    cotangent = heavy_noise(seeds[11], (TOKENS, D), 1.0, 24.0, ((0, 128),), (0, 1, 128, 5.5))
    return dict(tokens=tokens, lengths=lengths, attention_gain=attention_gain, query_weight=query_weight, key_weight=key_weight, value_weight=value_weight, out_weight=out_weight, feedforward_gain=feedforward_gain, gate_weight=gate_weight, up_weight=up_weight, down_weight=down_weight, cotangent=cotangent)


EPSILON = 1e-05
ROPE_BASE = 10000.0
NEGATIVE = -1e+30
HIGH = lax.Precision.HIGHEST

@jax.custom_vjp
def low(v):
    return lax.optimization_barrier(v.astype(jnp.bfloat16)).astype(jnp.float32)

@jax.custom_vjp
def low_back(v):
    return v

def low_keep(v):
    return (low(v), None)

def low_pass(kept, grad):
    return (grad,)

def back_keep(v):
    return (v, None)

def back_low(kept, grad):
    return (low(grad),)
low.defvjp(low_keep, low_pass)
low_back.defvjp(back_keep, back_low)

def matmul(left, right):
    return jnp.dot(left, right, precision=HIGH, preferred_element_type=jnp.float32)

def layout(lengths_row):
    ends = jnp.cumsum(lengths_row).astype(jnp.int32)
    starts = (ends - lengths_row).astype(jnp.int32)
    index = jnp.arange(GROUP_TOK, dtype=jnp.int32)
    segment = lax.optimization_barrier(jnp.sum((index[:, None] >= ends[None, :]).astype(jnp.int32), axis=1)).astype(jnp.int32)
    slots = jnp.arange(NSEG, dtype=jnp.int32)
    offset = lax.optimization_barrier(jnp.sum(jnp.where(segment[:, None] == slots[None, :], starts[None, :], 0), axis=1)).astype(jnp.int32)
    return (segment, (index - offset).astype(jnp.int32))

def angles(position, width):
    half = width // 2
    freq = jnp.exp(jnp.arange(half, dtype=jnp.float32) * (-2.0 * math.log(ROPE_BASE) / width))
    angle = position.astype(jnp.float32)[:, None] * freq[None, :]
    return (jnp.cos(angle)[:, None, :], jnp.sin(angle)[:, None, :])

def rotate(values, cosine, sine):
    half = values.shape[-1] // 2
    first = values[..., :half]
    second = values[..., half:]
    return jnp.concatenate([first * cosine - second * sine, second * cosine + first * sine], axis=-1)

def attention_group(items):
    query, key, value, segment, position = items
    cosine, sine = angles(position, HD)
    index = jnp.arange(GROUP_TOK, dtype=jnp.int32)
    allowed = (segment[:, None] == segment[None, :]) & (index[None, :] <= index[:, None])
    rotated_query = low(rotate(query, cosine, sine)).reshape(GROUP_TOK, KV_HEADS, HEADS // KV_HEADS, HD)
    rotated_key = low(rotate(key, cosine, sine))
    raw = low_back(jnp.einsum('qkgd,skd->kgqs', rotated_query, rotated_key, precision=HIGH))
    scores = jnp.where(allowed, raw * (1.0 / math.sqrt(HD)), NEGATIVE)
    top = lax.optimization_barrier(jnp.max(scores, axis=3, keepdims=True))
    expo = jnp.exp(scores - top)
    probs = expo / lax.optimization_barrier(jnp.sum(expo, axis=3, keepdims=True))
    mixed = jnp.einsum('kgqs,skd->qkgd', low(probs), value, precision=HIGH)
    return mixed.reshape(GROUP_TOK, HEADS * HD)

def normalize(values, gain):
    return values * lax.rsqrt(lax.optimization_barrier(jnp.mean(values * values, axis=1, keepdims=True)) + EPSILON) * gain

def forward(tokens, attention_gain, query_weight, key_weight, value_weight, out_weight, feedforward_gain, gate_weight, up_weight, down_weight, segment, position):
    normed_one = low(normalize(tokens, attention_gain))
    query = low_back(matmul(normed_one, query_weight))
    key = low_back(matmul(normed_one, key_weight))
    value = low(low_back(matmul(normed_one, value_weight)))
    heads = lax.map(jax.checkpoint(attention_group), (query.reshape(GROUPS, GROUP_TOK, HEADS, HD), key.reshape(GROUPS, GROUP_TOK, KV_HEADS, HD), value.reshape(GROUPS, GROUP_TOK, KV_HEADS, HD), segment, position))
    heads = low(low_back(heads.reshape(TOKENS, HEADS * HD)))
    mixed = tokens + low_back(matmul(heads, out_weight))
    normed_two = low(normalize(mixed, feedforward_gain))
    gate = low_back(matmul(normed_two, gate_weight))
    up = low_back(matmul(normed_two, up_weight))
    hidden = low(jax.nn.silu(gate) * up)
    return mixed + matmul(hidden, down_weight)

def reference(tokens, lengths, attention_gain, query_weight, key_weight, value_weight, out_weight, feedforward_gain, gate_weight, up_weight, down_weight, cotangent):
    segment, position = jax.vmap(layout)(lengths)
    floats = [item.astype(jnp.float32) for item in (tokens, attention_gain, query_weight, key_weight, value_weight, out_weight, feedforward_gain, gate_weight, up_weight, down_weight)]

    def run(*params):
        return forward(*params, segment, position)
    output, pullback = jax.vjp(run, *floats)
    grads = pullback(cotangent.astype(jnp.float32))
    return (output.astype(jnp.bfloat16), grads[0].astype(jnp.bfloat16), grads[1], grads[2], grads[3], grads[4], grads[5], grads[6], grads[7], grads[8], grads[9])
```

```python
import functools
import math

import jax
import jax.numpy as jnp
from jax import lax
from jax.experimental import pallas as pl
from jax.experimental.pallas import tpu as pltpu
from jax.sharding import PartitionSpec as P

HD = 64
MESH = pl.DeviceIdType.MESH


def remote(src, dst, send, recv, device):
    return pltpu.make_async_remote_copy(
        src_ref=src, dst_ref=dst, send_sem=send, recv_sem=recv, device_id=device, device_id_type=MESH
    )


class Place:
    def __init__(self):
        dp = lax.axis_index("dp")
        tensor = lax.axis_index("tensor")
        self.zh, self.x, self.y = dp // 16, (dp // 4) % 4, dp % 4
        self.zl, self.c = tensor // 2, tensor % 2
        self.dp, self.tensor = dp, tensor

    def step(self, v, k):
        return lax.rem(v + k + 4, 4)

    def at(self, zh=None, x=None, y=None, zl=None, c=None):
        zh = self.zh if zh is None else zh
        x = self.x if x is None else x
        y = self.y if y is None else y
        zl = self.zl if zl is None else zl
        c = self.c if c is None else c
        return (zh * 16 + x * 4 + y, zl * 2 + c)

    def ring(self, axis, k):
        if axis == "x":
            return self.at(x=self.step(self.x, k))
        return self.at(y=self.step(self.y, k))

    def partner(self):
        return self.at(zh=1 - self.zh)


def greet(devices):
    barrier = pltpu.get_barrier_semaphore()
    for device in devices:
        pl.semaphore_signal(barrier, inc=1, device_id=device, device_id_type=MESH)
    pl.semaphore_wait(barrier, len(devices))


GATHER_SEMS = 48


class Gather:
    def __init__(self, place, own, far, full, send, recv, local):
        self.p, self.own, self.far, self.full = place, own, far, full
        self.send, self.recv, self.local = send, recv, local
        self.sent = []
        self.count = 0

    def _region(self, half, first, second, lo, hi, z):
        rows = pl.ds(32 * half + lo, hi - lo)
        x, y = (first, second) if half == 0 else (second, first)
        return self.full.at[z, x, y, rows]

    def _push(self, src, dst, device, came):
        k = self.count
        self.count += 1
        copy = remote(src, dst, self.send.at[k], self.recv.at[k], device)
        copy.start()
        self.sent.append(copy)
        landing = remote(came, came, self.send.at[k], self.recv.at[k], device)
        return landing.wait_recv

    def axes(self, half):
        p = self.p
        return (("x", p.x), ("y", p.y)) if half == 0 else (("y", p.y), ("x", p.x))

    def start(self):
        p = self.p
        self.wait_far = self._push(
            self.far, self.full.at[p.zh, p.x, p.y], p.partner(), self.full.at[1 - p.zh, p.x, p.y]
        )
        self.copy = pltpu.make_async_copy(self.own, self.full.at[p.zh, p.x, p.y], self.local)
        self.copy.start()
        self.one = {}
        for half in (0, 1):
            (ring, me), (_, other) = self.axes(half)
            rows = pl.ds(32 * half, 32)
            for way in (1, -1):
                self.one[half, way, 0] = self._push(
                    self.own.at[rows],
                    self._region(half, me, other, 0, 32, p.zh),
                    p.ring(ring, way),
                    self._region(half, p.step(me, -way), other, 0, 32, p.zh),
                )

    def after_far(self):
        p = self.p
        self.wait_far()
        self.copy.wait()
        for half in (0, 1):
            (ring, me), (_, other) = self.axes(half)
            for way in (1, -1):
                src = self._region(half, me, other, 0, 32, 1 - p.zh)
                self.one[half, way, 1] = self._push(
                    src, src, p.ring(ring, way),
                    self._region(half, p.step(me, -way), other, 0, 32, 1 - p.zh),
                )
        self.big = {}
        for half in (0, 1):
            self._second(half, 0)

    def _second(self, half, k):
        p = self.p
        (_, me), (ring, other) = self.axes(half)
        at = p.step(me, k)
        for way in (1, -1):
            src = self._region(half, at, other, 0, 32, slice(None))
            self.big[half, way, k] = self._push(
                src, src, p.ring(ring, way),
                self._region(half, at, p.step(other, -way), 0, 32, slice(None)),
            )

    def after_one(self):
        p = self.p
        self.two = {}
        for way in (1, -1):
            for half in (0, 1):
                (ring, me), (_, other) = self.axes(half)
                self.one[half, way, 0]()
                self.one[half, way, 1]()
                lo = 0 if way == 1 else 16
                src = self._region(half, p.step(me, -way), other, lo, lo + 16, slice(None))
                self.two[half, way] = self._push(
                    src, src, p.ring(ring, way),
                    self._region(half, p.step(me, 2), other, lo, lo + 16, slice(None)),
                )
                self._second(half, -way)

    def after_two(self):
        for half in (0, 1):
            for way in (1, -1):
                self.two[half, way]()
            self._second(half, 2)

    def after_big(self, k):
        p = self.p
        if k == 0:
            self.last = {}
        for way in (1, -1):
            for half in (0, 1):
                (_, me), (ring, other) = self.axes(half)
                at = p.step(me, k)
                self.big[half, way, k]()
                lo = 0 if way == 1 else 16
                src = self._region(half, at, p.step(other, -way), lo, lo + 16, slice(None))
                self.last[half, way, k] = self._push(
                    src, src, p.ring(ring, way),
                    self._region(half, at, p.step(other, 2), lo, lo + 16, slice(None)),
                )

    def finish(self):
        for wait in self.last.values():
            wait()
        for copy in self.sent:
            copy.wait_send()

    def neighbours(self):
        p = self.p
        return [p.partner()] + [p.ring(a, k) for a in "xy" for k in (1, -1)]

    def steps(self):
        yield self.start
        yield self.after_far
        yield self.after_one
        yield self.after_two
        for k in (0, -1, 1, 2):
            yield functools.partial(self.after_big, k)
        yield self.finish


REDUCE_SEMS = 104
LANES = (2, 1, -1, 0)


def reduce_buffers(columns):
    half = (2, 16, columns)
    return [
        pltpu.VMEM((2, 2, 4) + half, jnp.bfloat16),
        pltpu.VMEM((2, 2, 4, 2, 32, columns), jnp.bfloat16),
        pltpu.VMEM((2, 2) + half, jnp.bfloat16),
        pltpu.VMEM((2, 2, 2, 32, columns), jnp.bfloat16),
        pltpu.VMEM((2, 32, columns), jnp.bfloat16),
    ]


def add_into(dst, *parts):
    total = dst[...].astype(jnp.float32)
    for part in parts:
        total = total + part[...].astype(jnp.float32)
    dst[...] = total.astype(dst.dtype)


class Reduce:
    def __init__(self, place, full, buffers, out, send, recv, base=0):
        self.p, self.full, self.out = place, full, out
        self.b1, self.b2, self.c1, self.c2, self.d = buffers
        self.send, self.recv = send, recv
        self.sent = []
        self.count = base
        self.waits = {}

    _region = Gather._region
    axes = Gather.axes
    neighbours = Gather.neighbours

    def _push(self, key, src, dst, device):
        k = self.count
        self.count += 1
        copy = remote(src, dst, self.send.at[k], self.recv.at[k], device)
        copy.start()
        self.sent.append(copy)
        self.waits[key] = copy.wait_recv

    def lane_start(self, k):
        p, n = self.p, LANES.index(k)
        for half in (0, 1):
            (_, me), (ring, other) = self.axes(half)
            at = p.step(me, k)
            for w, way in enumerate((1, -1)):
                lo = 0 if way == 1 else 16
                self._push(
                    ("b1", half, w, n),
                    self._region(half, at, p.step(other, 2), lo, lo + 16, slice(None)),
                    self.b1.at[half, w, n], p.ring(ring, way),
                )
        for half in (0, 1):
            (_, me), (ring, other) = self.axes(half)
            at = p.step(me, k)
            for w, way in enumerate((1, -1)):
                lo = 16 if way == 1 else 0
                self._push(
                    ("b2", half, w, n),
                    self._region(half, at, p.step(other, way), lo, lo + 16, slice(None)),
                    self.b2.at[half, w, n, :, pl.ds(lo, 16)], p.ring(ring, way),
                )

    def lane_pass(self, k):
        p, n = self.p, LANES.index(k)
        for half in (0, 1):
            (_, me), (ring, other) = self.axes(half)
            at = p.step(me, k)
            for w, way in enumerate((1, -1)):
                lo = 0 if way == 1 else 16
                self.waits["b1", half, w, n]()
                src = self._region(half, at, p.step(other, way), lo, lo + 16, slice(None))
                add_into(src, self.b1.at[half, w, n])
                self._push(
                    ("b2x", half, w, n), src, self.b2.at[half, w, n, :, pl.ds(lo, 16)], p.ring(ring, way)
                )

    def lane_end(self, k):
        p, n = self.p, LANES.index(k)
        for half in (0, 1):
            (ring, me), (_, other) = self.axes(half)
            at = p.step(me, k)
            for w in (0, 1):
                self.waits["b2", half, w, n]()
                self.waits["b2x", half, w, n]()
            mine = self._region(half, at, other, 0, 32, slice(None))
            add_into(mine, self.b2.at[half, 0, n], self.b2.at[half, 1, n])
            if k == 2:
                for w, way in enumerate((1, -1)):
                    lo = 0 if way == 1 else 16
                    self._push(
                        ("c1", half, w), self._region(half, at, other, lo, lo + 16, slice(None)),
                        self.c1.at[half, w], p.ring(ring, way),
                    )
            elif k != 0:
                w, lo = (0, 16) if k == 1 else (1, 0)
                self._push(
                    ("c2", half, w), self._region(half, at, other, lo, lo + 16, slice(None)),
                    self.c2.at[half, w, :, pl.ds(lo, 16)], p.ring(ring, k),
                )

    def pass_one(self):
        p = self.p
        for half in (0, 1):
            (ring, me), (_, other) = self.axes(half)
            for w, way in enumerate((1, -1)):
                lo = 0 if way == 1 else 16
                self.waits["c1", half, w]()
                src = self._region(half, p.step(me, way), other, lo, lo + 16, slice(None))
                add_into(src, self.c1.at[half, w])
                self._push(("c2x", half, w), src, self.c2.at[half, w, :, pl.ds(lo, 16)], p.ring(ring, way))

    def end_one(self):
        p = self.p
        for half in (0, 1):
            (ring, me), (_, other) = self.axes(half)
            for w in (0, 1):
                self.waits["c2", half, w]()
                self.waits["c2x", half, w]()
            for z in (1 - p.zh, p.zh):
                mine = self._region(half, me, other, 0, 32, z)
                add_into(mine, self.c2.at[half, 0, z], self.c2.at[half, 1, z])
                if z is not p.zh:
                    self._push(("d", half), mine, self.d.at[half], p.partner())

    def finish(self):
        p = self.p
        for half in (0, 1):
            (_, me), (_, other) = self.axes(half)
            self.waits["d", half]()
            mine = self._region(half, me, other, 0, 32, p.zh)
            self.out[pl.ds(32 * half, 32)] = mine[...].astype(jnp.float32) + self.d[half].astype(jnp.float32)
        for copy in self.sent:
            copy.wait_send()

    def steps(self):
        for k in LANES:
            yield functools.partial(self.lane_start, k)
        for i, k in enumerate(LANES):
            yield functools.partial(self.lane_pass, k)
            if i:
                yield functools.partial(self.lane_end, LANES[i - 1])
        yield functools.partial(self.lane_end, 0)
        yield self.pass_one
        yield self.end_one
        yield self.finish


EPSILON = 1e-05
ROPE_BASE = 10000.0
NEGATIVE = -1e30


def layout(lengths_row, group_rows):
    ends = jnp.cumsum(lengths_row)
    starts = ends - lengths_row
    index = jnp.arange(group_rows, dtype=jnp.int32)
    segment = jnp.sum((index[:, None] >= ends[None, :]).astype(jnp.int32), axis=1)
    slots = jnp.arange(lengths_row.shape[0], dtype=jnp.int32)
    offset = jnp.sum(jnp.where(segment[:, None] == slots[None, :], starts[None, :], 0), axis=1)
    allowed = (segment[:, None] == segment[None, :]) & (index[None, :] <= index[:, None])
    return (index - offset, allowed)


def angles(position, width):
    half = width // 2
    freq = jnp.exp(jnp.arange(half, dtype=jnp.float32) * (-2.0 * math.log(ROPE_BASE) / width))
    angle = position.astype(jnp.float32)[:, None] * freq[None, :]
    return (jnp.cos(angle)[:, None, :], jnp.sin(angle)[:, None, :])


def rotate(values, cosine, sine):
    half = values.shape[-1] // 2
    first = values[..., :half]
    second = values[..., half:]
    return jnp.concatenate(
        [first * cosine - second * sine, second * cosine + first * sine], axis=-1
    )


def unrotate(values, cosine, sine):
    half = values.shape[-1] // 2
    first = values[..., :half]
    second = values[..., half:]
    return jnp.concatenate(
        [first * cosine + second * sine, second * cosine - first * sine], axis=-1
    )


def normalize(values):
    factor = lax.rsqrt(jnp.mean(values * values, axis=1, keepdims=True) + EPSILON)
    return (values * factor, factor)


def norm_back(unit_grad, unit, factor):
    return factor * (unit_grad - unit * jnp.mean(unit_grad * unit, axis=1, keepdims=True))


def times_transposed(left, right):
    return lax.dot_general(
        left, right, (((1,), (1,)), ((), ())), preferred_element_type=jnp.float32
    )


def transposed_times(left, right):
    return lax.dot_general(
        left, right, (((0,), (0,)), ((), ())), preferred_element_type=jnp.float32
    )


def masked_scores(query, key, allowed, factor):
    raw = jnp.einsum("qkgd,skd->kgqs", query, key, preferred_element_type=jnp.float32)
    return jnp.where(allowed, raw * factor, NEGATIVE)


def gather_kernel(own, full, send, recv, local):
    place = Place()
    gather = Gather(place, own, own, full, send, recv, local)
    greet(gather.neighbours())
    for step in gather.steps():
        step()


def gather_all(own):
    columns = own.shape[1]
    full = pl.pallas_call(
        gather_kernel,
        out_shape=jax.ShapeDtypeStruct((2, 4, 4, 64, columns), own.dtype),
        in_specs=[pl.BlockSpec(memory_space=pl.ANY)],
        out_specs=pl.BlockSpec(memory_space=pl.ANY),
        scratch_shapes=[
            pltpu.SemaphoreType.DMA((GATHER_SEMS,)),
            pltpu.SemaphoreType.DMA((GATHER_SEMS,)),
            pltpu.SemaphoreType.DMA,
        ],
        compiler_params=pltpu.CompilerParams(collective_id=0, has_side_effects=True),
    )(own)
    return full.reshape(2048, columns)


def reduce_kernel(full, out, work, b1, b2, c1, c2, d, send, recv, local):
    place = Place()
    copy = pltpu.make_async_copy(full, work, local)
    copy.start()
    reduce = Reduce(place, work, (b1, b2, c1, c2, d), out, send, recv)
    greet(reduce.neighbours())
    copy.wait()
    for step in reduce.steps():
        step()


def reduce_all(parts):
    columns = parts.shape[1]
    return pl.pallas_call(
        reduce_kernel,
        out_shape=jax.ShapeDtypeStruct((64, columns), jnp.float32),
        in_specs=[pl.BlockSpec(memory_space=pl.ANY)],
        out_specs=pl.BlockSpec(memory_space=pltpu.VMEM),
        scratch_shapes=[pltpu.VMEM((2, 4, 4, 64, columns), jnp.bfloat16)]
        + reduce_buffers(columns)
        + [
            pltpu.SemaphoreType.DMA((REDUCE_SEMS,)),
            pltpu.SemaphoreType.DMA((REDUCE_SEMS,)),
            pltpu.SemaphoreType.DMA,
        ],
        compiler_params=pltpu.CompilerParams(
            collective_id=1, has_side_effects=True, vmem_limit_bytes=63 * 2**20
        ),
    )(parts.reshape(2, 4, 4, 64, columns))


def shards(
    tokens,
    lengths,
    attention_gain,
    query_weight,
    key_weight,
    value_weight,
    out_weight,
    feedforward_gain,
    gate_weight,
    up_weight,
    down_weight,
    cotangent,
):
    rows = tokens.shape[0]
    group_rows = rows * lax.axis_size("tensor")
    factor = 1.0 / math.sqrt(HD)
    position, allowed = layout(lengths[0], group_rows)
    cosine, sine = angles(position, HD)
    inputs = tokens.astype(jnp.float32)
    gains = jnp.stack([attention_gain, feedforward_gain], axis=1)
    packed = jnp.concatenate(
        [query_weight, key_weight, value_weight, out_weight.T, gate_weight, up_weight, down_weight.T,
         jnp.pad(gains, ((0, 0), (0, 126)))], axis=1)
    full = gather_all(packed)
    query_full, key_full, value_full, out_full, gate_full, up_full, down_full, gains = jnp.split(
        full, (512, 576, 640, 1152, 2560, 3968, 5376), axis=1)
    gain_one, gain_two = gains[:, 0], gains[:, 1]
    unit_one, factor_one = normalize(inputs)
    normed_one = (unit_one * gain_one.astype(jnp.float32)).astype(jnp.bfloat16)
    group_one = lax.all_gather(normed_one, "tensor", axis=0, tiled=True)
    local_heads = query_full.shape[1] // HD
    local_groups = key_full.shape[1] // HD
    per_group = local_heads // local_groups
    query = jnp.dot(group_one, query_full, preferred_element_type=jnp.float32).reshape(
        group_rows, local_heads, HD
    )
    query = (
        rotate(query, cosine, sine)
        .astype(jnp.bfloat16)
        .reshape(group_rows, local_groups, per_group, HD)
    )
    key = jnp.dot(group_one, key_full, preferred_element_type=jnp.float32).reshape(
        group_rows, local_groups, HD
    )
    key = rotate(key, cosine, sine).astype(jnp.bfloat16)
    value = jnp.dot(group_one, value_full, preferred_element_type=jnp.float32).astype(jnp.bfloat16)
    value = value.reshape(group_rows, local_groups, HD)
    scores = masked_scores(query, key, allowed, factor)
    top = jnp.max(scores, axis=3, keepdims=True)
    expo = jnp.exp(scores - top)
    total = jnp.sum(expo, axis=3, keepdims=True)
    weights = (expo / total).astype(jnp.bfloat16)
    log_total = top + jnp.log(total)
    heads = jnp.einsum("kgqs,skd->qkgd", weights, value, preferred_element_type=jnp.float32)
    heads = heads.reshape(group_rows, local_heads * HD).astype(jnp.bfloat16)
    mixed = inputs + lax.psum_scatter(
        times_transposed(heads, out_full).astype(jnp.bfloat16),
        "tensor",
        scatter_dimension=0,
        tiled=True,
    ).astype(jnp.float32)
    unit_two, factor_two = normalize(mixed)
    normed_two = (unit_two * gain_two.astype(jnp.float32)).astype(jnp.bfloat16)
    group_two = lax.all_gather(normed_two, "tensor", axis=0, tiled=True)
    gate = jnp.dot(group_two, gate_full, preferred_element_type=jnp.float32)
    up = jnp.dot(group_two, up_full, preferred_element_type=jnp.float32)
    hidden = (jax.nn.silu(gate) * up).astype(jnp.bfloat16)
    output = (
        mixed
        + lax.psum_scatter(
            times_transposed(hidden, down_full).astype(jnp.bfloat16),
            "tensor",
            scatter_dimension=0,
            tiled=True,
        ).astype(jnp.float32)
    ).astype(jnp.bfloat16)
    cot_rows = lax.all_gather(cotangent, "tensor", axis=0, tiled=True)
    down_part = transposed_times(cot_rows, hidden)
    hidden_grad = jnp.dot(cot_rows, down_full, preferred_element_type=jnp.float32)
    sigmoid = jax.nn.sigmoid(gate)
    gate_act_grad = (hidden_grad * up * sigmoid * (1.0 + gate * (1.0 - sigmoid))).astype(
        jnp.bfloat16
    )
    up_act_grad = (hidden_grad * gate * sigmoid).astype(jnp.bfloat16)
    gate_part = transposed_times(group_two, gate_act_grad)
    up_part = transposed_times(group_two, up_act_grad)
    normed_two_grad = lax.psum_scatter(
        (
            times_transposed(gate_act_grad, gate_full) + times_transposed(up_act_grad, up_full)
        ).astype(jnp.bfloat16),
        "tensor",
        scatter_dimension=0,
        tiled=True,
    ).astype(jnp.float32)
    gain_two_part = jnp.sum(normed_two_grad * unit_two, axis=0)
    mixed_grad = cotangent.astype(jnp.float32) + norm_back(
        normed_two_grad * gain_two.astype(jnp.float32), unit_two, factor_two
    )
    attended_rows = lax.all_gather(mixed_grad.astype(jnp.bfloat16), "tensor", axis=0, tiled=True)
    heads_grad = jnp.dot(attended_rows, out_full, preferred_element_type=jnp.float32).astype(jnp.bfloat16)
    out_part = transposed_times(attended_rows, heads)
    heads_grad = heads_grad.reshape(group_rows, local_groups, per_group, HD)
    probs = jnp.exp(masked_scores(query, key, allowed, factor) - log_total)
    kept_weights = probs.astype(jnp.bfloat16)
    prob_grad = jnp.einsum("qkgd,skd->kgqs", heads_grad, value, preferred_element_type=jnp.float32)
    score_grad = probs * (prob_grad - jnp.sum(probs * prob_grad, axis=3, keepdims=True)) * factor
    score_grad = score_grad.astype(jnp.bfloat16)
    rotated_query_grad = jnp.einsum(
        "kgqs,skd->qkgd", score_grad, key, preferred_element_type=jnp.float32
    )
    rotated_key_grad = jnp.einsum(
        "kgqs,qkgd->skd", score_grad, query, preferred_element_type=jnp.float32
    )
    value_act_grad = jnp.einsum(
        "kgqs,qkgd->skd", kept_weights, heads_grad, preferred_element_type=jnp.float32
    )
    value_act_grad = value_act_grad.astype(jnp.bfloat16).reshape(group_rows, local_groups * HD)
    query_act_grad = unrotate(rotated_query_grad.reshape(group_rows, local_heads, HD), cosine, sine)
    query_act_grad = query_act_grad.astype(jnp.bfloat16).reshape(group_rows, local_heads * HD)
    key_act_grad = (
        unrotate(rotated_key_grad, cosine, sine)
        .astype(jnp.bfloat16)
        .reshape(group_rows, local_groups * HD)
    )
    query_part = transposed_times(group_one, query_act_grad)
    key_part = transposed_times(group_one, key_act_grad)
    value_part = transposed_times(group_one, value_act_grad)
    total_term = times_transposed(query_act_grad, query_full)
    total_term = total_term + times_transposed(key_act_grad, key_full)
    normed_one_grad = lax.psum_scatter(
        (total_term + times_transposed(value_act_grad, value_full)).astype(jnp.bfloat16),
        "tensor",
        scatter_dimension=0,
        tiled=True,
    ).astype(jnp.float32)
    gain_one_part = jnp.sum(normed_one_grad * unit_one, axis=0)
    input_grad = (
        mixed_grad + norm_back(normed_one_grad * gain_one.astype(jnp.float32), unit_one, factor_one)
    ).astype(jnp.bfloat16)
    gain_parts = jnp.pad(jnp.stack([gain_one_part, gain_two_part], axis=1), ((0, 0), (0, 126)))
    parts = [query_part, key_part, value_part, out_part, gate_part, up_part, down_part, gain_parts]
    summed = reduce_all(jnp.concatenate([part.astype(jnp.bfloat16) for part in parts], axis=1))
    query_grad, key_grad, value_grad, out_grad, gate_grad, up_grad, down_grad, gain_sums = jnp.split(
        summed, (512, 576, 640, 1152, 2560, 3968, 5376), axis=1)
    out_grad, down_grad = out_grad.T, down_grad.T
    gain_sums = lax.psum(gain_sums[:, :2], "tensor")
    attention_gain_grad, feedforward_gain_grad = gain_sums[:, 0], gain_sums[:, 1]
    return (
        output,
        input_grad,
        attention_gain_grad,
        query_grad,
        key_grad,
        value_grad,
        out_grad,
        feedforward_gain_grad,
        gate_grad,
        up_grad,
        down_grad,
    )


def solution(mesh):
    return jax.shard_map(
        shards,
        mesh=mesh,
        in_specs=(
            P(("dp", "tensor"), None),
            P("dp", None),
            P("dp"),
            P("dp", "tensor"),
            P("dp", "tensor"),
            P("dp", "tensor"),
            P("tensor", "dp"),
            P("dp"),
            P("dp", "tensor"),
            P("dp", "tensor"),
            P("tensor", "dp"),
            P(("dp", "tensor"), None),
        ),
        out_specs=(
            P(("dp", "tensor"), None),
            P(("dp", "tensor"), None),
            P("dp"),
            P("dp", "tensor"),
            P("dp", "tensor"),
            P("dp", "tensor"),
            P("tensor", "dp"),
            P("dp"),
            P("dp", "tensor"),
            P("dp", "tensor"),
            P("tensor", "dp"),
        ),
        check_vma=False,
    )
```

```python
import functools
import math

import jax
import jax.numpy as jnp
from jax import lax
from jax.experimental import pallas as pl
from jax.experimental.pallas import tpu as pltpu
from jax.sharding import PartitionSpec as P

HD = 64
EPSILON = 1e-05
ROPE_BASE = 10000.0
NEGATIVE = -1e30
MESH = pl.DeviceIdType.MESH


def remote(src, dst, send, recv, device):
    return pltpu.make_async_remote_copy(
        src_ref=src, dst_ref=dst, send_sem=send, recv_sem=recv, device_id=device, device_id_type=MESH
    )


class Place:
    def __init__(self):
        dp = lax.axis_index("dp")
        tensor = lax.axis_index("tensor")
        self.zh, self.x, self.y = dp // 16, (dp // 4) % 4, dp % 4
        self.zl, self.c = tensor // 2, tensor % 2
        self.dp, self.tensor = dp, tensor
        self.z = self.zh * 2 + self.zl

    def step(self, v, k):
        return lax.rem(v + k + 4, 4)

    def at(self, zh=None, x=None, y=None, zl=None, c=None):
        zh = self.zh if zh is None else zh
        x = self.x if x is None else x
        y = self.y if y is None else y
        zl = self.zl if zl is None else zl
        c = self.c if c is None else c
        return (zh * 16 + x * 4 + y, zl * 2 + c)

    def ring(self, axis, k):
        if axis == "x":
            return self.at(x=self.step(self.x, k))
        return self.at(y=self.step(self.y, k))

    def at_z(self, k):
        z = self.step(self.z, k)
        return self.at(zh=z // 2, zl=z % 2)

    def partner(self):
        return self.at(zh=1 - self.zh)


def greet(devices):
    barrier = pltpu.get_barrier_semaphore()
    for device in devices:
        pl.semaphore_signal(barrier, inc=1, device_id=device, device_id_type=MESH)
    pl.semaphore_wait(barrier, len(devices))


GATHER_SEMS = 48


class Gather:
    def __init__(self, place, own, far, full, send, recv, local):
        self.p, self.own, self.far, self.full = place, own, far, full
        self.send, self.recv, self.local = send, recv, local
        self.sent = []
        self.count = 0

    def _region(self, half, first, second, lo, hi, z):
        rows = pl.ds(32 * half + lo, hi - lo)
        x, y = (first, second) if half == 0 else (second, first)
        return self.full.at[z, x, y, rows]

    def _push(self, src, dst, device, came):
        k = self.count
        self.count += 1
        copy = remote(src, dst, self.send.at[k], self.recv.at[k], device)
        copy.start()
        self.sent.append(copy)
        landing = remote(came, came, self.send.at[k], self.recv.at[k], device)
        return landing.wait_recv

    def axes(self, half):
        p = self.p
        return (("x", p.x), ("y", p.y)) if half == 0 else (("y", p.y), ("x", p.x))

    def start(self):
        p = self.p
        self.wait_far = self._push(
            self.far, self.full.at[p.zh, p.x, p.y], p.partner(), self.full.at[1 - p.zh, p.x, p.y]
        )
        self.copy = pltpu.make_async_copy(self.own, self.full.at[p.zh, p.x, p.y], self.local)
        self.copy.start()
        self.one = {}
        for half in (0, 1):
            (ring, me), (_, other) = self.axes(half)
            rows = pl.ds(32 * half, 32)
            for way in (1, -1):
                self.one[half, way, 0] = self._push(
                    self.own.at[rows],
                    self._region(half, me, other, 0, 32, p.zh),
                    p.ring(ring, way),
                    self._region(half, p.step(me, -way), other, 0, 32, p.zh),
                )

    def after_far(self):
        p = self.p
        self.wait_far()
        self.copy.wait()
        for half in (0, 1):
            (ring, me), (_, other) = self.axes(half)
            for way in (1, -1):
                src = self._region(half, me, other, 0, 32, 1 - p.zh)
                self.one[half, way, 1] = self._push(
                    src, src, p.ring(ring, way),
                    self._region(half, p.step(me, -way), other, 0, 32, 1 - p.zh),
                )
        self.big = {}
        for half in (0, 1):
            self._second(half, 0)

    def _second(self, half, k):
        p = self.p
        (_, me), (ring, other) = self.axes(half)
        at = p.step(me, k)
        for way in (1, -1):
            src = self._region(half, at, other, 0, 32, slice(None))
            self.big[half, way, k] = self._push(
                src, src, p.ring(ring, way),
                self._region(half, at, p.step(other, -way), 0, 32, slice(None)),
            )

    def after_one(self):
        p = self.p
        self.two = {}
        for way in (1, -1):
            for half in (0, 1):
                (ring, me), (_, other) = self.axes(half)
                self.one[half, way, 0]()
                self.one[half, way, 1]()
                lo = 0 if way == 1 else 16
                src = self._region(half, p.step(me, -way), other, lo, lo + 16, slice(None))
                self.two[half, way] = self._push(
                    src, src, p.ring(ring, way),
                    self._region(half, p.step(me, 2), other, lo, lo + 16, slice(None)),
                )
                self._second(half, -way)

    def after_two(self):
        for half in (0, 1):
            for way in (1, -1):
                self.two[half, way]()
            self._second(half, 2)

    def after_big(self, k):
        p = self.p
        if k == 0:
            self.last = {}
        for way in (1, -1):
            for half in (0, 1):
                (_, me), (ring, other) = self.axes(half)
                at = p.step(me, k)
                self.big[half, way, k]()
                lo = 0 if way == 1 else 16
                src = self._region(half, at, p.step(other, -way), lo, lo + 16, slice(None))
                self.last[half, way, k] = self._push(
                    src, src, p.ring(ring, way),
                    self._region(half, at, p.step(other, 2), lo, lo + 16, slice(None)),
                )

    def arrive(self):
        for wait in self.last.values():
            wait()

    def drain(self):
        for copy in self.sent:
            copy.wait_send()

    def neighbours(self):
        p = self.p
        return [p.partner()] + [p.ring(a, k) for a in "xy" for k in (1, -1)]

    def steps(self):
        yield self.start
        yield self.after_far
        yield self.after_one
        yield self.after_two
        for k in (0, -1, 1, 2):
            yield functools.partial(self.after_big, k)
        yield self.finish


REDUCE_SEMS = 104
LANES = (2, 1, -1, 0)


def reduce_buffers(columns):
    half = (2, 16, columns)
    return [
        pltpu.VMEM((2, 2, 4) + half, jnp.bfloat16),
        pltpu.VMEM((2, 2, 4, 2, 32, columns), jnp.bfloat16),
        pltpu.VMEM((2, 2) + half, jnp.bfloat16),
        pltpu.VMEM((2, 2, 2, 32, columns), jnp.bfloat16),
        pltpu.VMEM((2, 32, columns), jnp.bfloat16),
    ]


def add_into(dst, *parts):
    total = dst[...].astype(jnp.float32)
    for part in parts:
        total = total + part[...].astype(jnp.float32)
    dst[...] = total.astype(dst.dtype)


class Reduce:
    def __init__(self, place, full, buffers, out, send, recv, base=0):
        self.p, self.full, self.out = place, full, out
        self.b1, self.b2, self.c1, self.c2, self.d = buffers
        self.send, self.recv = send, recv
        self.sent = []
        self.count = base
        self.waits = {}

    _region = Gather._region
    axes = Gather.axes
    neighbours = Gather.neighbours

    def _push(self, key, src, dst, device):
        k = self.count
        self.count += 1
        copy = remote(src, dst, self.send.at[k], self.recv.at[k], device)
        copy.start()
        self.sent.append(copy)
        self.waits[key] = copy.wait_recv

    def lane_start(self, k):
        p, n = self.p, LANES.index(k)
        for half in (0, 1):
            (_, me), (ring, other) = self.axes(half)
            at = p.step(me, k)
            for w, way in enumerate((1, -1)):
                lo = 0 if way == 1 else 16
                self._push(
                    ("b1", half, w, n),
                    self._region(half, at, p.step(other, 2), lo, lo + 16, slice(None)),
                    self.b1.at[half, w, n], p.ring(ring, way),
                )
        for half in (0, 1):
            (_, me), (ring, other) = self.axes(half)
            at = p.step(me, k)
            for w, way in enumerate((1, -1)):
                lo = 16 if way == 1 else 0
                self._push(
                    ("b2", half, w, n),
                    self._region(half, at, p.step(other, way), lo, lo + 16, slice(None)),
                    self.b2.at[half, w, n, :, pl.ds(lo, 16)], p.ring(ring, way),
                )

    def lane_pass(self, k):
        p, n = self.p, LANES.index(k)
        for half in (0, 1):
            (_, me), (ring, other) = self.axes(half)
            at = p.step(me, k)
            for w, way in enumerate((1, -1)):
                lo = 0 if way == 1 else 16
                self.waits["b1", half, w, n]()
                src = self._region(half, at, p.step(other, way), lo, lo + 16, slice(None))
                add_into(src, self.b1.at[half, w, n])
                self._push(
                    ("b2x", half, w, n), src, self.b2.at[half, w, n, :, pl.ds(lo, 16)], p.ring(ring, way)
                )

    def lane_end(self, k):
        p, n = self.p, LANES.index(k)
        for half in (0, 1):
            (ring, me), (_, other) = self.axes(half)
            at = p.step(me, k)
            for w in (0, 1):
                self.waits["b2", half, w, n]()
                self.waits["b2x", half, w, n]()
            mine = self._region(half, at, other, 0, 32, slice(None))
            add_into(mine, self.b2.at[half, 0, n], self.b2.at[half, 1, n])
            if k == 2:
                for w, way in enumerate((1, -1)):
                    lo = 0 if way == 1 else 16
                    self._push(
                        ("c1", half, w), self._region(half, at, other, lo, lo + 16, slice(None)),
                        self.c1.at[half, w], p.ring(ring, way),
                    )
            elif k != 0:
                w, lo = (0, 16) if k == 1 else (1, 0)
                self._push(
                    ("c2", half, w), self._region(half, at, other, lo, lo + 16, slice(None)),
                    self.c2.at[half, w, :, pl.ds(lo, 16)], p.ring(ring, k),
                )

    def pass_one(self):
        p = self.p
        for half in (0, 1):
            (ring, me), (_, other) = self.axes(half)
            for w, way in enumerate((1, -1)):
                lo = 0 if way == 1 else 16
                self.waits["c1", half, w]()
                src = self._region(half, p.step(me, way), other, lo, lo + 16, slice(None))
                add_into(src, self.c1.at[half, w])
                self._push(("c2x", half, w), src, self.c2.at[half, w, :, pl.ds(lo, 16)], p.ring(ring, way))

    def end_one(self):
        p = self.p
        for half in (0, 1):
            (ring, me), (_, other) = self.axes(half)
            for w in (0, 1):
                self.waits["c2", half, w]()
                self.waits["c2x", half, w]()
            for z in (1 - p.zh, p.zh):
                mine = self._region(half, me, other, 0, 32, z)
                add_into(mine, self.c2.at[half, 0, z], self.c2.at[half, 1, z])
                if z is not p.zh:
                    self._push(("d", half), mine, self.d.at[half], p.partner())

    def finish(self):
        p = self.p
        for half in (0, 1):
            (_, me), (_, other) = self.axes(half)
            self.waits["d", half]()
            mine = self._region(half, me, other, 0, 32, p.zh)
            self.out[pl.ds(32 * half, 32)] = mine[...].astype(jnp.float32) + self.d[half].astype(jnp.float32)

    def steps(self):
        for k in LANES:
            yield functools.partial(self.lane_start, k)
        for i, k in enumerate(LANES):
            yield functools.partial(self.lane_pass, k)
            if i:
                yield functools.partial(self.lane_end, LANES[i - 1])
        yield functools.partial(self.lane_end, 0)
        yield self.pass_one
        yield self.end_one
        yield self.finish


ORDER = (0, -1, 1, 2)


class Pushes:
    def __init__(self, send, recv):
        self.send, self.recv, self.count, self.sent = send, recv, 0, []

    def push(self, src, dst, device, came=None):
        k = self.count
        self.count += 1
        copy = remote(src, dst, self.send.at[k], self.recv.at[k], device)
        copy.start()
        self.sent.append(copy)
        if came is None:
            return copy.wait_recv
        return remote(came, came, self.send.at[k], self.recv.at[k], device).wait_recv

    def drain(self):
        for copy in self.sent:
            copy.wait_send()
        self.sent = []


class Column:
    def __init__(self, place, full, pushes):
        self.p, self.full, self.pushes = place, full, pushes

    def at(self, k, c):
        return self.full.at[self.p.step(self.p.z, k) * 2 + c]

    def start(self, own):
        p, push = self.p, self.pushes.push
        dst = self.at(0, p.c)
        self.near = {w: push(own, dst, p.at_z(w), self.at(-w, p.c)) for w in (1, -1)}
        self.core = {0: push(own, dst, p.at(c=1 - p.c), self.at(0, 1 - p.c))}

    def after_near(self):
        p, push = self.p, self.pushes.push
        self.far = {}
        for w in (1, -1):
            self.near[w]()
            lo = 0 if w == 1 else 64
            src = self.at(-w, p.c).at[pl.ds(lo, 64)]
            self.far[w] = push(src, src, p.at_z(w), self.at(2, p.c).at[pl.ds(lo, 64)])
        for w in (1, -1):
            src = self.at(-w, p.c)
            self.core[-w] = push(src, src, p.at(c=1 - p.c), self.at(-w, 1 - p.c))

    def after_far(self):
        p, push = self.p, self.pushes.push
        for w in (1, -1):
            self.far[w]()
        src = self.at(2, p.c)
        self.core[2] = push(src, src, p.at(c=1 - p.c), self.at(2, 1 - p.c))

    def finish(self):
        for k in (0, -1, 1, 2):
            self.core[k]()


def everyone(p):
    return (
        [p.partner(), p.at(c=1 - p.c)]
        + [p.ring(a, k) for a in "xy" for k in (1, -1)]
        + [p.at_z(k) for k in (1, -1)]
    )


def f32(x):
    return x.astype(jnp.float32)


def bf16(x):
    return x.astype(jnp.bfloat16)


def dot_nn(a, b):
    return lax.dot_general(a, b, (((1,), (0,)), ((), ())), preferred_element_type=jnp.float32)


def dot_nt(a, b):
    return lax.dot_general(a, b, (((1,), (1,)), ((), ())), preferred_element_type=jnp.float32)


def dot_tn(a, b):
    return lax.dot_general(a, b, (((0,), (0,)), ((), ())), preferred_element_type=jnp.float32)


def halves_swapped(v):
    lane = lax.broadcasted_iota(jnp.int32, v.shape, 1)
    return jnp.where(lane % 64 < 32, pltpu.roll(v, v.shape[1] - 32, 1), pltpu.roll(v, 32, 1))


def root(v):
    return lax.rsqrt(jnp.mean(v * v, axis=1, keepdims=True) + EPSILON)


def softmax_pair(q_pair, key, value, bias):
    outs, lses = [], []
    for h in range(2):
        q = q_pair[:, 64 * h : 64 * h + 64]
        rows, sums = [], []
        for lo, hi in ((0, 256), (256, 512)):
            s = dot_nt(q[lo:hi], key[:hi]) + bias[lo:hi, :hi]
            top = jnp.max(s, axis=1, keepdims=True)
            e = jnp.exp(s - top)
            total = jnp.sum(e, axis=1, keepdims=True)
            rows.append(dot_nn(bf16(e * (1.0 / total)), value[:hi]))
            sums.append(top + jnp.log(total))
        outs.append(jnp.concatenate(rows, axis=0))
        lses.append(jnp.concatenate(sums, axis=0))
    return jnp.concatenate(outs, axis=1), lses


class ColumnSum:
    def __init__(self, place, parts, core_in, near_in, far_in, pushes):
        self.p, self.parts, self.core_in, self.near_in, self.far_in = place, parts, core_in, near_in, far_in
        self.pushes = pushes
        self.core, self.near, self.far = {}, {}, {}

    def ready(self, k):
        p = self.p
        z = p.step(p.z, k)
        self.core[k] = self.pushes.push(self.parts.at[2 * z + 1 - p.c], self.core_in.at[z], p.at(c=1 - p.c))

    def pass_on(self, k):
        p, push = self.p, self.pushes.push
        z = p.step(p.z, k)
        mine = self.parts.at[2 * z + p.c]
        self.core[k]()
        if k == 2:
            mine[...] = bf16(f32(mine[...]) + f32(self.core_in[z]))
            for w, way in enumerate((1, -1)):
                self.near[way] = push(mine.at[pl.ds(64 * w, 64)], self.near_in.at[w], p.at_z(way))
        elif k:
            w = 0 if k == 1 else 1
            self.near[k]()
            lo = 64 * w
            total = f32(mine[...]) + f32(self.core_in[z])
            mine[...] = bf16(total)
            mine[lo : lo + 64] = bf16(total[lo : lo + 64] + f32(self.near_in[w]))
            self.far[k] = push(mine, self.far_in.at[w], p.at_z(k))

    def total(self):
        p = self.p
        self.pass_on(0)
        self.far[1]()
        self.far[-1]()
        return (
            f32(self.parts[2 * p.z + p.c]) + f32(self.core_in[p.z]) + f32(self.far_in[0]) + f32(self.far_in[1])
        )


def wide(ref, lo, size):
    return ref[:, :, :, :, pl.ds(lo, size)].reshape(2048, size)


def rows_of(ref, d, first=0, size=None):
    size = ref.shape[-1] if size is None else size
    return ref[d // 4, d % 4, :, :, first : first + size].reshape(256, size)


def loop(n, body):
    lax.fori_loop(0, n, lambda i, _: (body(i), 0)[1], 0)


def forward_kernel(
    tokens, cot, seg_c, seg_r, cosine, sine, w1_own, w2_own, w3_own, w4_own,
    w1_out, w2_out, g3_out, g4_out, n1, q_out, kv_out, heads_out, lse_out, bias_out, output, mixed_grad,
    w1, w2, w3, w4, tok, cot_all, n2_all, n2_own, part, cbuf, zbuf, mixed_s, act, hid,
    out_part, out_core, out_near, out_far, d_part, d_core, d_near, d_far,
    sems, ex_s, ex_r, loc,
):
    p = Place()
    core, side = p.at(c=1 - p.c), p.at(zl=1 - p.zl)
    here, there = p.tensor, (1 - p.zl) * 2 + p.c
    g1 = Gather(p, w1_own, w1_own, w1, sems.at[0], sems.at[1], loc.at[0])
    g2 = Gather(p, w2_own, w2_own, w2, sems.at[2], sems.at[3], loc.at[1])
    g3 = Gather(p, w3_own.at[p.zh], w3_own.at[1 - p.zh], w3, sems.at[4], sems.at[5], loc.at[2])
    g4 = Gather(p, w4_own.at[p.zh], w4_own.at[1 - p.zh], w4, sems.at[6], sems.at[7], loc.at[3])
    ex = Pushes(ex_s, ex_r)
    greet(everyone(p))
    g1.start()
    tok[here] = tokens[...]
    tok_side = ex.push(tokens, tok.at[here], side, tok.at[there])
    tok_core = ex.push(tokens, tok.at[here], core, tok.at[p.zl * 2 + 1 - p.c])
    g1.after_far()
    g2.start()
    row = lax.broadcasted_iota(jnp.int32, (512, 512), 0)
    col = lax.broadcasted_iota(jnp.int32, (512, 512), 1)
    bias_out[...] = jnp.where((seg_c[...] == seg_r[...]) & (col <= row), 0.0, NEGATIVE)
    v = f32(tokens[...])
    n1[pl.ds(128 * here, 128)] = bf16(v * root(v))
    g1.after_one()
    g2.after_far()
    g1.after_two()
    tok_side()
    tok_far = ex.push(tok.at[there], tok.at[there], core, tok.at[(1 - p.zl) * 2 + 1 - p.c])
    cots = Column(p, cot_all, ex)
    cots.at(0, p.c)[...] = cot[...]
    cots.start(cot)
    for k in ORDER:
        g1.after_big(k)
        if k == 0:
            g2.after_one()
        if k == -1:
            g2.after_two()
            g3.start()
    tok_core()
    tok_far()
    for b in (there, p.zl * 2 + 1 - p.c, (1 - p.zl) * 2 + 1 - p.c):
        v = f32(tok[b])
        n1[pl.ds(128 * b, 128)] = bf16(v * root(v))
    g1.arrive()
    g2.after_big(0)
    g3.after_far()
    keep = [pltpu.make_async_copy(w1, w1_out, loc.at[4])]
    keep[0].start()
    for j in range(5):
        v = dot_nn(n1[...], wide(w1, 128 * j, 128))
        r = v * cosine[...] + halves_swapped(v) * sine[...]
        if j < 4:
            q_out[j] = bf16(r) * 0.125
        else:
            lane = lax.broadcasted_iota(jnp.int32, v.shape, 1)
            kv_out[...] = bf16(jnp.where(lane < 64, r, v))
    g2.after_big(-1)
    g2.after_big(1)
    key, value = kv_out[:, :64], kv_out[:, 64:]
    for j in range(4):
        out, lses = softmax_pair(q_out[j], key, value, bias_out)
        heads_out[:, 128 * j : 128 * j + 128] = bf16(out)
        for h in range(2):
            lse_out[:, 2 * j + h : 2 * j + h + 1] = lses[h]
        if j == 0:
            g2.after_big(2)
            cots.after_near()
        if j == 2:
            g3.after_one()
    g2.arrive()
    keep.append(pltpu.make_async_copy(w2, w2_out, loc.at[5]))
    keep[1].start()
    for d in range(8):
        part[:, :, 256 * d : 256 * d + 256] = bf16(dot_nt(heads_out[...], rows_of(w2, d))).reshape(4, 128, 256)
    near = [ex.push(part.at[z * 2 + 1 - p.c], cbuf.at[z], core) for z in range(2)]
    cots.after_far()
    near[0]()
    near[1]()
    part[there] = bf16(f32(part[there]) + f32(cbuf[1 - p.zl]))
    got = ex.push(part.at[there], zbuf, side)
    mixed = f32(tokens[...]) + f32(part[here]) + f32(cbuf[p.zl])
    g3.after_two()
    g4.start()
    got()
    mixed = mixed + f32(zbuf[...])
    mixed_s[...] = mixed
    n2_own[...] = bf16(mixed * root(mixed))
    n2 = Column(p, n2_all, ex)
    n2.at(0, p.c)[...] = n2_own[...]
    n2.start(n2_own)
    g3.after_big(0)
    g4.after_far()
    n2.after_near()
    g3.after_big(-1)
    g3.after_big(1)
    g4.after_one()
    n2.after_far()
    g3.after_big(2)
    g4.after_two()
    g4.after_big(0)
    g3.arrive()

    def chunk(ref, k):
        z = p.step(p.z, k)
        return ref.at[pl.ds(2 * z, 2)]

    def gate_up(k):
        z = p.step(p.z, k)
        rows = chunk(n2_all, k)

        def body(n):
            x = rows[...].reshape(256, 2048)
            gate = dot_nn(x, wide(w3, pl.multiple_of(256 * n, 256), 256))
            up = dot_nn(x, wide(w3, pl.multiple_of(768 + 256 * n, 256), 256))
            s = 1.0 / (1.0 + jnp.exp(-gate))
            silu = gate * s
            at = pl.ds(pl.multiple_of(256 * z, 256), 256)
            hid[at, pl.ds(pl.multiple_of(256 * n, 256), 256)] = bf16(silu * up)
            act[at, pl.ds(pl.multiple_of(256 * n, 256), 256)] = bf16(up * s * (1.0 + gate * (1.0 - s)))
            act[at, pl.ds(pl.multiple_of(768 + 256 * n, 256), 256)] = bf16(silu)

        loop(3, body)

    n2.core[0]()
    gate_up(0)
    g4.after_big(-1)
    n2.core[-1]()
    gate_up(-1)
    g4.after_big(1)
    n2.core[1]()
    gate_up(1)
    g4.after_big(2)
    n2.core[2]()
    gate_up(2)
    cots.finish()
    g4.arrive()

    outs = ColumnSum(p, out_part, out_core, out_near, out_far, ex)
    grads = ColumnSum(p, d_part, d_core, d_near, d_far, ex)

    def back(k):
        z = p.step(p.z, k)
        at = pl.ds(pl.multiple_of(256 * z, 256), 256)
        rows = chunk(cot_all, k)

        def body(n):
            g = dot_nn(rows[...].reshape(256, 2048), wide(w4, pl.multiple_of(256 * n, 256), 256))
            for lo in (0, 768):
                c = pl.ds(pl.multiple_of(lo + 256 * n, 256), 256)
                act[at, c] = bf16(g * f32(act[at, c]))

        loop(3, body)

        def deep(d):
            c = pl.ds(pl.multiple_of(256 * d, 256), 256)
            g = dot_nt(act[at], rows_of(w3, d))
            chunk(d_part, k)[:, :, c] = bf16(g).reshape(2, 128, 256)
            o = dot_nt(hid[at], rows_of(w4, d))
            chunk(out_part, k)[:, :, c] = bf16(o).reshape(2, 128, 256)

        loop(8, deep)
        grads.ready(k)
        outs.ready(k)

    before = None
    for k in (2, 1, -1, 0):
        back(k)
        if before is not None:
            grads.pass_on(before)
            outs.pass_on(before)
        before = k
    g3.drain()
    g4.drain()

    def deep3(d):
        c = pl.ds(pl.multiple_of(256 * d, 256), 256)
        x = n2_all[:, :, c].reshape(1024, 256)
        w3[d // 4, d % 4] = bf16(dot_tn(x, act[...])).reshape(4, 64, 1536)

    def deep4(d):
        c = pl.ds(pl.multiple_of(256 * d, 256), 256)
        x = cot_all[:, :, c].reshape(1024, 256)
        w4[d // 4, d % 4] = bf16(dot_tn(x, hid[...])).reshape(4, 64, 768)

    loop(8, deep4)
    keep.append(pltpu.make_async_copy(w4, g4_out, loc.at[6]))
    keep[2].start()
    loop(8, deep3)
    keep.append(pltpu.make_async_copy(w3, g3_out, loc.at[7]))
    keep[3].start()
    mixed = mixed_s[...]
    factor = root(mixed)
    unit = mixed * factor
    grad = grads.total()
    mixed_grad[...] = f32(cot[...]) + factor * (grad - unit * jnp.mean(grad * unit, axis=1, keepdims=True))
    output[...] = bf16(mixed + outs.total())
    for copy in keep:
        copy.wait()
    g1.drain()
    g2.drain()
    ex.drain()


def forward(tokens, cot, seg, cosine, sine, w1, w2, w3, w4):
    any_, vmem = pl.BlockSpec(memory_space=pl.ANY), pl.BlockSpec(memory_space=pltpu.VMEM)
    shape = lambda s, t=jnp.bfloat16: jax.ShapeDtypeStruct(s, t)
    dma, held = pltpu.SemaphoreType.DMA, lambda *s: pltpu.VMEM(s, jnp.bfloat16)
    sums = [held(8, 128, 2048), held(4, 128, 2048), held(2, 64, 2048), held(2, 128, 2048)]
    return pl.pallas_call(
        forward_kernel,
        out_shape=[
            shape((2, 4, 4, 64, 640)), shape((2, 4, 4, 64, 512)),
            shape((2, 4, 4, 64, 1536)), shape((2, 4, 4, 64, 768)),
            shape((512, 2048)), shape((4, 512, 128)), shape((512, 128)), shape((512, 512)),
            shape((512, 8), jnp.float32), shape((512, 512), jnp.float32),
            shape((128, 2048)), shape((128, 2048), jnp.float32),
        ],
        in_specs=[vmem] * 6 + [any_] * 4,
        out_specs=[any_] * 4 + [vmem] * 8,
        scratch_shapes=[
            held(2, 4, 4, 64, 640), held(2, 4, 4, 64, 512), held(2, 4, 4, 64, 1536), held(2, 4, 4, 64, 768),
            held(4, 128, 2048), held(8, 128, 2048), held(8, 128, 2048), held(128, 2048),
            held(4, 128, 2048), held(2, 128, 2048), held(128, 2048), pltpu.VMEM((128, 2048), jnp.float32),
            held(1024, 1536), held(1024, 768),
        ] + sums + sums + [dma((8, GATHER_SEMS)), dma((48,)), dma((48,)), dma((8,))],
        compiler_params=pltpu.CompilerParams(collective_id=0, has_side_effects=True, vmem_limit_bytes=63 * 2**20),
    )(tokens, cot, seg[:, None], seg[None, :], cosine, sine, w1, w2, w3, w4)


class SplitReduce(Reduce):
    def end_one(self):
        p = self.p
        for half in (0, 1):
            (ring, me), (_, other) = self.axes(half)
            for w in (0, 1):
                self.waits["c2", half, w]()
                self.waits["c2x", half, w]()
            for z in (1 - p.zh, p.zh):
                mine = self._region(half, me, other, 0, 32, z)
                add_into(mine, self.c2.at[half, 0, z], self.c2.at[half, 1, z])
                if z is not p.zh:
                    self._push(("d", half), mine, self.d.at[half], p.partner())
            self.out[p.zh, pl.ds(32 * half, 32)] = f32(self._region(half, me, other, 0, 32, p.zh)[...])

    def finish(self):
        p = self.p
        for half in (0, 1):
            self.waits["d", half]()
            self.out[1 - p.zh, pl.ds(32 * half, 32)] = f32(self.d[half])


def head_back(q, key, value, g, lse, bias):
    dq, dk, dv = [], None, None
    for lo, hi in ((256, 512), (0, 256)):
        s = dot_nt(q[lo:hi], key[:hi]) + bias[lo:hi, :hi]
        probs = jnp.exp(s - lse[lo:hi])
        dp = dot_nt(g[lo:hi], value[:hi])
        ds = bf16(probs * (dp - jnp.sum(probs * dp, axis=1, keepdims=True)))
        dq.insert(0, dot_nn(ds, key[:hi]))
        k_part, v_part = dot_tn(ds, q[lo:hi]), dot_tn(bf16(probs), g[lo:hi])
        if dk is None:
            dk, dv = k_part, v_part
        else:
            dk = jnp.concatenate([dk[:256] + k_part, dk[256:]], axis=0)
            dv = jnp.concatenate([dv[:256] + v_part, dv[256:]], axis=0)
    return jnp.concatenate(dq, axis=0), dk, dv


def backward_kernel(
    tokens, mixed_grad, n1, q_all, kv, heads, lse, bias, cosine, sine, w1_own, w3_own, w1_in, w2_in, g3_in, g4_in,
    input_grad, r1, r2, r3, r4, gains,
    w1, w2, g3, g4, att, dheads, act, dk_s, dv_s, part, cbuf, zbuf, gain_in,
    b1a, b1b, b1c, b1d, b1e, b2a, b2b, b2c, b2d, b2e, b3a, b3b, b3c, b3d, b3e, b4a, b4b, b4c, b4d, b4e,
    sems, ex_s, ex_r, loc,
):
    p = Place()
    core, side = p.at(c=1 - p.c), p.at(zl=1 - p.zl)
    here, there = p.tensor, (1 - p.zl) * 2 + p.c
    loads = [
        pltpu.make_async_copy(src, dst, loc.at[i])
        for i, (src, dst) in enumerate(((g4_in, g4), (g3_in, g3), (w2_in, w2), (w1_in, w1)))
    ]
    for copy in loads:
        copy.start()
    ex = Pushes(ex_s, ex_r)
    s1 = Reduce(p, w1, (b1a, b1b, b1c, b1d, b1e), r1, sems.at[0], sems.at[1])
    s2 = Reduce(p, w2, (b2a, b2b, b2c, b2d, b2e), r2, sems.at[2], sems.at[3])
    s3 = SplitReduce(p, g3, (b3a, b3b, b3c, b3d, b3e), r3, sems.at[4], sems.at[5])
    s4 = SplitReduce(p, g4, (b4a, b4b, b4c, b4d, b4e), r4, sems.at[6], sems.at[7])
    greet([p.partner(), core, side] + [p.ring(a, k) for a in "xy" for k in (1, -1)])
    att[here] = bf16(mixed_grad[...])
    at_side = ex.push(att.at[here], att.at[here], side, att.at[there])
    at_core = ex.push(att.at[here], att.at[here], core, att.at[p.zl * 2 + 1 - p.c])
    loads[0].wait()
    for k in LANES:
        s4.lane_start(k)
    loads[1].wait()
    for k in LANES:
        s3.lane_start(k)
    loads[2].wait()
    loads[3].wait()
    at_side()
    at_far = ex.push(att.at[there], att.at[there], core, att.at[(1 - p.zl) * 2 + 1 - p.c])
    for k in LANES:
        s4.lane_pass(k)
    at_core()
    at_far()
    for j in range(2):
        x = att[...].reshape(512, 2048)
        dheads[:, 256 * j : 256 * j + 256] = bf16(dot_nn(x, wide(w2, 256 * j, 256)))

    def deep2(d):
        c = pl.ds(pl.multiple_of(256 * d, 256), 256)
        w2[d // 4, d % 4] = bf16(dot_tn(att[:, :, c].reshape(512, 256), heads[...])).reshape(4, 64, 512)

    loop(8, deep2)
    for k in LANES:
        s4.lane_end(k)
    for k in LANES:
        s2.lane_start(k)
    for k in LANES[:2]:
        s3.lane_pass(k)
    key, value = kv[:, :64], kv[:, 64:]
    for j in range(4):
        dqs = []
        for h in range(2):
            at = slice(128 * j + 64 * h, 128 * j + 64 * h + 64)
            dq, dk, dv = head_back(
                q_all[j, :, 64 * h : 64 * h + 64], key, value, dheads[:, at], lse[:, 2 * j + h : 2 * j + h + 1], bias
            )
            dqs.append(dq)
            if j + h == 0:
                dk_s[...] = dk
                dv_s[...] = dv
            else:
                dk_s[...] += dk
                dv_s[...] += dv
        v = jnp.concatenate(dqs, axis=1) * 0.125
        act[:, 128 * j : 128 * j + 128] = bf16(v * cosine[...] - halves_swapped(v) * sine[...])
        if j == 0:
            s4.pass_one()
            s3.lane_pass(LANES[2])
            s3.lane_pass(LANES[3])
        if j == 1:
            s3.lane_end(LANES[0])
            s3.lane_end(LANES[1])
        if j == 2:
            s3.lane_end(LANES[2])
            s3.lane_end(LANES[3])
    v = jnp.concatenate([dk_s[...], dv_s[...]], axis=1)
    lane = lax.broadcasted_iota(jnp.int32, v.shape, 1)
    act[:, 512:640] = bf16(jnp.where(lane < 64, v * cosine[...] - halves_swapped(v) * sine[...], v))

    def deep(d):
        c = pl.ds(pl.multiple_of(256 * d, 256), 256)
        part[:, :, c] = bf16(dot_nt(act[...], rows_of(w1, d))).reshape(4, 128, 256)

    loop(8, deep)
    near = [ex.push(part.at[z * 2 + 1 - p.c], cbuf.at[z], core) for z in range(2)]
    for wait in near:
        wait()
    part[there] = bf16(f32(part[there]) + f32(cbuf[1 - p.zl]))
    got = ex.push(part.at[there], zbuf, side)

    def deep1(d):
        c = pl.ds(pl.multiple_of(256 * d, 256), 256)
        w1[d // 4, d % 4] = bf16(dot_tn(n1[:, c], act[...])).reshape(4, 64, 640)

    loop(8, deep1)
    for k in LANES:
        s1.lane_start(k)
    s4.end_one()
    for k in LANES:
        s2.lane_pass(k)
    s3.pass_one()
    for k in LANES:
        s2.lane_end(k)
    for k in LANES:
        s1.lane_pass(k)
    s2.pass_one()
    s3.end_one()
    for k in LANES:
        s1.lane_end(k)
    got()
    v = f32(tokens[...])
    factor = root(v)
    unit = v * factor
    grad = f32(part[here]) + f32(cbuf[p.zl]) + f32(zbuf[...])
    input_grad[...] = bf16(
        mixed_grad[...] + factor * (grad - unit * jnp.mean(grad * unit, axis=1, keepdims=True))
    )
    s2.end_one()
    s1.pass_one()
    s4.finish()
    s3.finish()
    two = jnp.zeros((64, 1), jnp.float32)
    for z in range(2):
        two = two + jnp.sum(f32(w3_own[z]) * r3[z], axis=1, keepdims=True)
    s1.end_one()
    s2.finish()
    s1.finish()
    one = jnp.sum(f32(w1_own[...]) * r1[...], axis=1, keepdims=True)
    lane = lax.broadcasted_iota(jnp.int32, (64, 128), 1)
    gains[...] = jnp.where(lane == 0, one, two)
    wait = ex.push(gains, gain_in.at[0], core)
    wait()
    gain_in[1] = gains[...] + gain_in[0]
    wait = ex.push(gain_in.at[1], gain_in.at[2], side)
    for copy in (*s1.sent, *s2.sent, *s3.sent, *s4.sent):
        copy.wait_send()
    wait()
    ex.drain()
    gains[...] = gain_in[1] + gain_in[2]


def backward(tokens, mixed_grad, n1, q, kv, heads, lse, bias, cosine, sine, w1_own, w3_own, w1, w2, g3, g4):
    any_, vmem = pl.BlockSpec(memory_space=pl.ANY), pl.BlockSpec(memory_space=pltpu.VMEM)
    full = lambda *s: jax.ShapeDtypeStruct(s, jnp.float32)
    dma, held = pltpu.SemaphoreType.DMA, lambda *s: pltpu.VMEM(s, jnp.bfloat16)
    return pl.pallas_call(
        backward_kernel,
        out_shape=[
            jax.ShapeDtypeStruct((128, 2048), jnp.bfloat16),
            full(64, 640), full(64, 512), full(2, 64, 1536), full(2, 64, 768), full(64, 128),
        ],
        in_specs=[vmem] * 12 + [any_] * 4,
        out_specs=[vmem] * 6,
        scratch_shapes=[
            held(2, 4, 4, 64, 640), held(2, 4, 4, 64, 512), held(2, 4, 4, 64, 1536), held(2, 4, 4, 64, 768),
            held(4, 128, 2048), held(512, 512), held(512, 640),
            pltpu.VMEM((512, 64), jnp.float32), pltpu.VMEM((512, 64), jnp.float32),
            held(4, 128, 2048), held(2, 128, 2048), held(128, 2048), pltpu.VMEM((3, 64, 128), jnp.float32),
        ]
        + reduce_buffers(640) + reduce_buffers(512) + reduce_buffers(1536) + reduce_buffers(768)
        + [dma((8, 64)), dma((16,)), dma((16,)), dma((4,))],
        compiler_params=pltpu.CompilerParams(collective_id=1, has_side_effects=True, vmem_limit_bytes=63 * 2**20),
    )(tokens, mixed_grad, n1, q, kv, heads, lse, bias, cosine, sine, w1_own, w3_own, w1, w2, g3, g4)


def halve(v):
    return jnp.pad(v.reshape(64, 2, 704), ((0, 0), (0, 0), (0, 64))).transpose(1, 0, 2)


def scaled(gain, weight):
    return (gain.astype(jnp.float32)[:, None] * weight.astype(jnp.float32)).astype(jnp.bfloat16)


def packed(attention_gain, feedforward_gain, query_weight, key_weight, value_weight, out_weight, gate_weight, up_weight, down_weight):
    first = scaled(attention_gain, jnp.concatenate([query_weight, key_weight, value_weight], axis=1))
    gate, up = scaled(feedforward_gain, gate_weight), scaled(feedforward_gain, up_weight)
    third = jnp.concatenate([halve(gate), halve(up)], axis=2)
    return first, out_weight.T, third, halve(down_weight.T)


def layout(lengths_row, rows):
    ends = jnp.cumsum(lengths_row)
    starts = ends - lengths_row
    index = jnp.arange(rows, dtype=jnp.int32)
    segment = jnp.sum((index[:, None] >= ends[None, :]).astype(jnp.int32), axis=1)
    slots = jnp.arange(lengths_row.shape[0], dtype=jnp.int32)
    offset = jnp.sum(jnp.where(segment[:, None] == slots[None, :], starts[None, :], 0), axis=1)
    return segment, index - offset


def angles(position):
    freq = jnp.exp(jnp.arange(32, dtype=jnp.float32) * (-2.0 * math.log(ROPE_BASE) / HD))
    angle = position.astype(jnp.float32)[:, None] * freq[None, :]
    cosine, sine = jnp.cos(angle), jnp.sin(angle)
    return jnp.tile(cosine, (1, 4)), jnp.tile(jnp.concatenate([-sine, sine], axis=1), (1, 2))


def shards(
    tokens,
    lengths,
    attention_gain,
    query_weight,
    key_weight,
    value_weight,
    out_weight,
    feedforward_gain,
    gate_weight,
    up_weight,
    down_weight,
    cotangent,
):
    segment, position = layout(lengths[0], 512)
    cosine, sine = angles(position)
    w1, w2, w3, w4 = packed(
        attention_gain, feedforward_gain, query_weight, key_weight, value_weight, out_weight, gate_weight, up_weight,
        down_weight,
    )
    w1_all, w2_all, g3, g4, n1, q, kv, heads, lse, bias, output, mixed_grad = forward(
        tokens, cotangent, segment, cosine, sine, w1, w2, w3, w4
    )
    input_grad, r1, r2, r3, r4, gains = backward(
        tokens, mixed_grad, n1, q, kv, heads, lse, bias, cosine, sine, w1, w3, w1_all, w2_all, g3, g4
    )
    one, two = attention_gain.astype(jnp.float32), feedforward_gain.astype(jnp.float32)
    r1 = r1 * one[:, None]
    units = lambda v: v[:, :, :704].transpose(1, 0, 2).reshape(64, 1408)
    return (
        output,
        input_grad,
        gains[:, 0] / one,
        r1[:, :512],
        r1[:, 512:576],
        r1[:, 576:],
        r2.T,
        gains[:, 1] / two,
        units(r3) * two[:, None],
        units(r3[:, :, 768:]) * two[:, None],
        units(r4).T,
    )


def solution(mesh):
    return jax.shard_map(
        shards,
        mesh=mesh,
        in_specs=(
            P(("dp", "tensor"), None),
            P("dp", None),
            P("dp"),
            P("dp", "tensor"),
            P("dp", "tensor"),
            P("dp", "tensor"),
            P("tensor", "dp"),
            P("dp"),
            P("dp", "tensor"),
            P("dp", "tensor"),
            P("tensor", "dp"),
            P(("dp", "tensor"), None),
        ),
        out_specs=(
            P(("dp", "tensor"), None),
            P(("dp", "tensor"), None),
            P("dp"),
            P("dp", "tensor"),
            P("dp", "tensor"),
            P("dp", "tensor"),
            P("tensor", "dp"),
            P("dp"),
            P("dp", "tensor"),
            P("dp", "tensor"),
            P("tensor", "dp"),
        ),
        check_vma=False,
    )
```

```python
import functools
import math

import jax
import jax.numpy as jnp
from jax import lax
from jax.experimental import pallas as pl
from jax.experimental.pallas import tpu as pltpu
from jax.sharding import PartitionSpec as P

HD = 64
EPSILON = 1e-05
ROPE_BASE = 10000.0
NEGATIVE = -1e30
PLAN = (
    4, 48, 5, 55, 54, 0, 1, 2, 50, 51, 6, 3, 8, 10, 15, 26, 37, 7, 16, 12, 9, 11, 49, 56, 59, 52, 17, 53, 13,
    18, 19, 21, 27, 62, 14, 66, 67, 23, 20, 28, 38, 68, 57, 24, 22, 69, 30, 70, 25, 32, 72, 58, 60, 29, 71, 73,
    34, 31, 64, 75, 61, 65, 33, 74, 77, 39, 63, 35, 76, 80, 83, 40, 41, 43, 78, 36, 42, 87, 44, 81, 45, 85, 46,
    84, 88, 79, 47, 82, 106, 86, 89, 107, 108, 90, 94, 100, 110, 91, 109, 101, 95, 97, 92, 111, 112, 113, 114,
    115, 98, 93, 119, 96, 122, 99, 103, 131, 134, 123, 120, 132, 125, 102, 116, 104, 124, 121, 133, 135, 126,
    142, 143, 153, 147, 150, 136, 144, 117, 137, 105, 159, 160, 164, 173, 170, 176, 179, 139, 138, 161, 140,
    148, 162, 118, 163, 180, 165, 185, 188, 171, 181, 194, 166, 191, 168, 154, 186, 127, 128, 189, 172, 141,
    195, 177, 206, 192, 174, 145, 151, 187, 155, 167, 129, 190, 196, 178, 193, 175, 182, 146, 152, 197, 169,
    183, 149, 156, 198, 157, 130, 205, 184, 200, 199, 201, 203, 158, 204, 202,
)
MESH = pl.DeviceIdType.MESH


def remote(src, dst, send, recv, device):
    return pltpu.make_async_remote_copy(
        src_ref=src, dst_ref=dst, send_sem=send, recv_sem=recv, device_id=device, device_id_type=MESH
    )


class Place:
    def __init__(self):
        dp = lax.axis_index("dp")
        tensor = lax.axis_index("tensor")
        self.zh, self.x, self.y = dp // 16, (dp // 4) % 4, dp % 4
        self.zl, self.c = tensor // 2, tensor % 2
        self.dp, self.tensor = dp, tensor
        self.z = self.zh * 2 + self.zl

    def step(self, v, k):
        return lax.rem(v + k + 4, 4)

    def at(self, zh=None, x=None, y=None, zl=None, c=None):
        zh = self.zh if zh is None else zh
        x = self.x if x is None else x
        y = self.y if y is None else y
        zl = self.zl if zl is None else zl
        c = self.c if c is None else c
        return (zh * 16 + x * 4 + y, zl * 2 + c)

    def ring(self, axis, k):
        if axis == "x":
            return self.at(x=self.step(self.x, k))
        return self.at(y=self.step(self.y, k))

    def at_z(self, k):
        z = self.step(self.z, k)
        return self.at(zh=z // 2, zl=z % 2)

    def partner(self):
        return self.at(zh=1 - self.zh)


def greet(devices, meanwhile):
    barrier = pltpu.get_barrier_semaphore()
    for device in devices:
        pl.semaphore_signal(barrier, inc=1, device_id=device, device_id_type=MESH)
    meanwhile()
    pl.semaphore_wait(barrier, len(devices))


def column(v):
    return jnp.sum(jnp.where(diagonal(), v.astype(jnp.float32), 0.0), axis=1, keepdims=True)


def row(v):
    return jnp.sum(jnp.where(diagonal(), v, 0.0), axis=0, keepdims=True)


def diagonal():
    return lax.broadcasted_iota(jnp.int32, (64, 64), 0) == lax.broadcasted_iota(jnp.int32, (64, 64), 1)


def starts(lengths, index):
    end, first = 0, jnp.zeros_like(index)
    for i in range(3):
        end = end + lengths[0, i]
        first = jnp.where(index >= end, end, first)
    return first


WAYS = (1, -1)
ORDER = (0, -1, 1, 2)
LANES = (2, 1, -1, 0)
SLOT = {2: 0, 1: 1, -1: 2, 0: 3}
GATHER_SEMS = 48
REDUCE_SEMS = 64


class Pushes:
    def __init__(self, send, recv):
        self.send, self.recv, self.count, self.sent = send, recv, 0, []

    def push(self, src, dst, device, came=None):
        k = self.count
        self.count += 1
        copy = remote(src, dst, self.send.at[k], self.recv.at[k], device)
        copy.start()
        self.sent.append(copy)
        if came is None:
            return copy
        return remote(came, came, self.send.at[k], self.recv.at[k], device)

    def drain(self, keep=0):
        last = len(self.sent) - keep
        for copy in self.sent[:last]:
            copy.wait_send()
        self.sent = self.sent[last:]


class Tasks:
    def __init__(self):
        self.all = {}

    def add(self, name, do, need=None, after=(), rank=0):
        self.all[name] = (do, need or (lambda: []), tuple(after), rank)

    def run(self, order):
        names = list(self.all)
        left = set(names)
        for name in [names[i] for i in order]:
            do, need, after, _ = self.all[name]
            left.remove(name)
            assert not left.intersection(after)
            for copy in need():
                copy.wait_recv()
            do()
        assert not left


def halves(p):
    return ((0, "x", p.x, "y", p.y), (1, "y", p.y, "x", p.x))


def region(full, half, first, second, lo, hi, z):
    rows = pl.ds(32 * half + lo, hi - lo)
    x, y = (first, second) if half == 0 else (second, first)
    return full.at[z, x, y, rows]


BOTH = slice(None)


class Gather(Pushes):
    def __init__(self, place, own, far, full, send, recv, local):
        super().__init__(send, recv)
        self.p, self.own, self.far, self.full, self.local = place, own, far, full, local
        self.one, self.two, self.big, self.last = {}, {}, {}, {}

    def to_partner(self):
        p = self.p
        self.wait_far = self.push(
            self.far, self.full.at[p.zh, p.x, p.y], p.partner(), self.full.at[1 - p.zh, p.x, p.y]
        )
        self.copy = pltpu.make_async_copy(self.own, self.full.at[p.zh, p.x, p.y], self.local)
        self.copy.start()

    def first(self, src, z, n):
        p = self.p
        for half, ring, me, _, other in halves(p):
            for way in WAYS:
                self.one[half, way, n] = self.push(
                    src.at[pl.ds(32 * half, 32)],
                    region(self.full, half, me, other, 0, 32, z),
                    p.ring(ring, way),
                    region(self.full, half, p.step(me, -way), other, 0, 32, z),
                )

    def near(self):
        self.first(self.own, self.p.zh, 0)

    def after_far(self):
        p = self.p
        self.first(self.full.at[1 - p.zh, p.x, p.y], 1 - p.zh, 1)
        self.copy.wait()
        for half in (0, 1):
            self.second(half, 0)

    def second(self, half, k):
        p = self.p
        _, _, me, ring, other = halves(p)[half]
        at = p.step(me, k)
        for way in WAYS:
            src = region(self.full, half, at, other, 0, 32, BOTH)
            self.big[half, way, k] = self.push(
                src, src, p.ring(ring, way), region(self.full, half, at, p.step(other, -way), 0, 32, BOTH)
            )

    def after_one(self, way):
        p = self.p
        for half, ring, me, _, other in halves(p):
            lo = 0 if way == 1 else 16
            src = region(self.full, half, p.step(me, -way), other, lo, lo + 16, BOTH)
            self.two[half, way] = self.push(
                src, src, p.ring(ring, way), region(self.full, half, p.step(me, 2), other, lo, lo + 16, BOTH)
            )
        for half in (0, 1):
            self.second(half, -way)

    def after_two(self):
        for half in (0, 1):
            self.second(half, 2)

    def after_big(self, k):
        p = self.p
        for way in WAYS:
            for half, _, me, ring, other in halves(p):
                at = p.step(me, k)
                lo = 0 if way == 1 else 16
                src = region(self.full, half, at, p.step(other, -way), lo, lo + 16, BOTH)
                self.last[half, way, k] = self.push(
                    src, src, p.ring(ring, way), region(self.full, half, at, p.step(other, 2), lo, lo + 16, BOTH)
                )

    def steps(self, t, name, rank, far_after=(), near_after=(), next_after=(), then_after=()):
        part = functools.partial
        pairs = [(half, way) for half in (0, 1) for way in WAYS]
        t.add(name + "_Z", self.to_partner, after=far_after, rank=rank)
        t.add(name + "_N", self.near, after=(name + "_Z",) + tuple(near_after), rank=rank)
        t.add(name + "_F", self.after_far, lambda: [self.wait_far], (name + "_N",) + next_after, rank)
        for way in WAYS:
            t.add(
                name + "_O%d" % way, part(self.after_one, way),
                lambda way=way: [self.one[half, way, n] for half in (0, 1) for n in (0, 1)], (name + "_F",) + then_after,
                rank,
            )
        t.add(
            name + "_T", self.after_two, lambda: [self.two[pair] for pair in pairs], (name + "_O1", name + "_O-1"), rank
        )
        for k, before in ((0, "_F"), (-1, "_O1"), (1, "_O-1"), (2, "_T")):
            t.add(
                name + "_B%d" % k, part(self.after_big, k),
                lambda k=k: [self.big[pair + (k,)] for pair in pairs], (name + before,), rank,
            )
        t.add(
            name + "_D", lambda: None, lambda: list(self.last.values()), [name + "_B%d" % k for k in ORDER], rank
        )


def reduce_buffers(columns):
    half = (2, 16, columns)
    return [
        pltpu.VMEM((2, 2, 4) + half, jnp.bfloat16),
        pltpu.VMEM((2, 2, 4, 2, 32, columns), jnp.bfloat16),
        pltpu.VMEM((2, 2) + half, jnp.bfloat16),
        pltpu.VMEM((2, 2, 2, 32, columns), jnp.bfloat16),
        pltpu.VMEM((2, 32, columns), jnp.bfloat16),
    ]


def add_into(dst, *parts):
    total = dst[...].astype(jnp.float32)
    for part in parts:
        total = total + part[...].astype(jnp.float32)
    dst[...] = total.astype(dst.dtype)


class Reduce(Pushes):
    def __init__(self, place, full, buffers, out, send, recv, split):
        super().__init__(send, recv)
        self.p, self.full, self.out, self.split = place, full, out, split
        self.b1, self.b2, self.c1, self.c2, self.d = buffers
        self.came = {}

    def lane_start(self, k):
        p, n = self.p, LANES.index(k)
        for half, _, me, ring, other in halves(p):
            at = p.step(me, k)
            for w, way in enumerate(WAYS):
                lo = 16 * w
                self.came["b1", half, w, n] = self.push(
                    region(self.full, half, at, p.step(other, 2), lo, lo + 16, BOTH),
                    self.b1.at[half, w, n], p.ring(ring, way),
                )
        for half, _, me, ring, other in halves(p):
            at = p.step(me, k)
            for w, way in enumerate(WAYS):
                lo = 16 - 16 * w
                self.came["b2", half, w, n] = self.push(
                    region(self.full, half, at, p.step(other, way), lo, lo + 16, BOTH),
                    self.b2.at[half, w, n, :, pl.ds(lo, 16)], p.ring(ring, way),
                )

    def lane_pass(self, k):
        p, n = self.p, LANES.index(k)
        for half, _, me, ring, other in halves(p):
            at = p.step(me, k)
            for w, way in enumerate(WAYS):
                lo = 16 * w
                src = region(self.full, half, at, p.step(other, way), lo, lo + 16, BOTH)
                add_into(src, self.b1.at[half, w, n])
                self.came["b2x", half, w, n] = self.push(
                    src, self.b2.at[half, w, n, :, pl.ds(lo, 16)], p.ring(ring, way)
                )

    def lane_end(self, k):
        p, n = self.p, LANES.index(k)
        for half, ring, me, _, other in halves(p):
            at = p.step(me, k)
            add_into(region(self.full, half, at, other, 0, 32, BOTH), self.b2.at[half, 0, n], self.b2.at[half, 1, n])
            if k == 2:
                for w, way in enumerate(WAYS):
                    lo = 16 * w
                    self.came["c1", half, w] = self.push(
                        region(self.full, half, at, other, lo, lo + 16, BOTH), self.c1.at[half, w], p.ring(ring, way)
                    )
            elif k != 0:
                w, lo = (0, 16) if k == 1 else (1, 0)
                self.came["c2", half, w] = self.push(
                    region(self.full, half, at, other, lo, lo + 16, BOTH),
                    self.c2.at[half, w, :, pl.ds(lo, 16)], p.ring(ring, k),
                )

    def pass_one(self):
        p = self.p
        for half, ring, me, _, other in halves(p):
            for w, way in enumerate(WAYS):
                lo = 16 * w
                src = region(self.full, half, p.step(me, way), other, lo, lo + 16, BOTH)
                add_into(src, self.c1.at[half, w])
                self.came["c2x", half, w] = self.push(src, self.c2.at[half, w, :, pl.ds(lo, 16)], p.ring(ring, way))

    def end_one(self):
        p = self.p
        for half, _, me, _, other in halves(p):
            mine = region(self.full, half, me, other, 0, 32, 1 - p.zh)
            add_into(mine, self.c2.at[half, 0, 1 - p.zh], self.c2.at[half, 1, 1 - p.zh])
            self.came["d", half] = self.push(mine, self.d.at[half], p.partner())
        for half, _, me, _, other in halves(p):
            mine = region(self.full, half, me, other, 0, 32, p.zh)
            add_into(mine, self.c2.at[half, 0, p.zh], self.c2.at[half, 1, p.zh])

    def finish(self):
        p = self.p
        for half, _, me, _, other in halves(p):
            rows = pl.ds(32 * half, 32)
            mine = f32(region(self.full, half, me, other, 0, 32, p.zh)[...])
            if self.split:
                self.out[p.zh, rows] = mine
                self.out[1 - p.zh, rows] = f32(self.d[half])
            else:
                self.out[rows] = mine + f32(self.d[half])

    def steps(self, t, name, rank, start_after):
        part = functools.partial
        four = [(half, w) for half in (0, 1) for w in (0, 1)]
        for n, k in enumerate(LANES):
            at = str(k)
            t.add(name + "_S" + at, part(self.lane_start, k), after=start_after, rank=rank)
            t.add(
                name + "_P" + at, part(self.lane_pass, k),
                lambda n=n: [self.came[("b1",) + f + (n,)] for f in four], (name + "_S" + at,), rank,
            )
            t.add(
                name + "_E" + at, part(self.lane_end, k),
                lambda n=n: [self.came[(b,) + f + (n,)] for f in four for b in ("b2", "b2x")], (name + "_P" + at,), rank,
            )
        t.add(
            name + "_Q", self.pass_one, lambda: [self.came[("c1",) + f] for f in four],
            (name + "_E2", name + "_E1", name + "_E-1"), rank,
        )
        t.add(
            name + "_R", self.end_one, lambda: [self.came[(c,) + f] for f in four for c in ("c2", "c2x")],
            (name + "_Q", name + "_E0"), rank,
        )
        t.add(name + "_D", self.finish, lambda: [self.came["d", half] for half in (0, 1)], (name + "_R",), rank)


class Column:
    def __init__(self, place, full, pushes):
        self.p, self.full, self.push = place, full, pushes.push
        self.near, self.far, self.core = {}, {}, {}

    def at(self, k, c, h=None):
        block = self.full.at[2 * SLOT[k] + c]
        return block if h is None else block.at[pl.ds(64 * h, 64)]

    def to_core(self, k, h):
        p = self.p
        src = self.at(k, p.c, h)
        self.core[k, h] = self.push(src, src, p.at(c=1 - p.c), self.at(k, 1 - p.c, h))

    def start(self, h):
        p = self.p
        src = self.at(0, p.c, h)
        for w in WAYS:
            dst = self.at(-w, p.c, h)
            self.near[h, w] = self.push(src, dst, p.at_z(w), dst)
        self.to_core(0, h)

    def after_near(self, h):
        p = self.p
        w = WAYS[h]
        src = self.at(-w, p.c, h)
        dst = self.at(2, p.c, h)
        self.far[h] = self.push(src, dst, p.at_z(w), dst)
        for k in WAYS:
            self.to_core(k, h)

    def steps(self, t, name, rank, start_after):
        part = functools.partial
        for h in (0, 1):
            i = str(h)
            t.add(name + "_S" + i, part(self.start, h), after=start_after[h], rank=rank)
            t.add(
                name + "_N" + i, part(self.after_near, h), lambda h=h: [self.near[h, w] for w in WAYS],
                (name + "_S" + i,), rank,
            )
            t.add(name + "_F" + i, part(self.to_core, 2, h), lambda h=h: [self.far[h]], (name + "_N" + i,), rank)
        for k, before in ((0, "_S"), (-1, "_N"), (1, "_N"), (2, "_F")):
            t.add(
                name + "_C%d" % k, lambda: None, lambda k=k: [self.core[k, h] for h in (0, 1)],
                (name + before + "0", name + before + "1"), rank,
            )


class ColumnSum:
    def __init__(self, place, parts, core_in, near_in, far_in, pushes):
        self.p, self.parts, self.core_in, self.near_in, self.far_in = place, parts, core_in, near_in, far_in
        self.push = pushes.push
        self.core, self.near, self.far = {}, {}, {}

    def ready(self, k):
        p = self.p
        self.core[k] = self.push(self.parts[k].at[1 - p.c], self.core_in.at[SLOT[k]], p.at(c=1 - p.c))

    def after_core(self, k):
        p = self.p
        mine = self.parts[k].at[p.c]
        add_into(mine, self.core_in.at[SLOT[k]])
        if k == 2:
            for w, way in enumerate(WAYS):
                self.near[way] = self.push(mine.at[pl.ds(64 * w, 64)], self.near_in.at[w], p.at_z(way))
        else:
            w = 0 if k == 1 else 1
            free = pl.ds(64 - 64 * w, 64)
            self.far[k, 0] = self.push(mine.at[free], self.far_in.at[w, free], p.at_z(k))

    def after_near(self, k):
        p = self.p
        w = 0 if k == 1 else 1
        rest = pl.ds(64 * w, 64)
        mine = self.parts[k].at[p.c, rest]
        add_into(mine, self.near_in.at[w])
        self.far[k, 1] = self.push(mine, self.far_in.at[w, rest], p.at_z(k))

    def total(self, rows):
        p = self.p
        return (
            f32(self.parts[0].at[p.c][rows]) + f32(self.core_in.at[SLOT[0]][rows])
            + f32(self.far_in.at[0][rows]) + f32(self.far_in.at[1][rows])
        )

    def steps(self, t, name, rank, ready, after=()):
        part = functools.partial
        for k in (2, 1, -1):
            t.add(name + "_P%d" % k, part(self.after_core, k), lambda k=k: [self.core[k]], (ready[k],) + after, rank)
        for k in WAYS:
            t.add(
                name + "_A%d" % k, part(self.after_near, k), lambda k=k: [self.near[k]],
                (name + "_P2", name + "_P%d" % k), rank,
            )

    def arrived(self):
        return [self.core[0]] + [self.far[k, i] for k in WAYS for i in (0, 1)]


def everyone(p):
    return (
        [p.partner(), p.at(c=1 - p.c)]
        + [p.ring(a, k) for a in "xy" for k in (1, -1)]
        + [p.at_z(k) for k in (1, -1)]
        + [p.at(zl=1 - p.zl, c=1 - p.c)]
    )


def f32(x):
    return x.astype(jnp.float32)


def bf16(x):
    return x.astype(jnp.bfloat16)


def dot_nn(a, b):
    return lax.dot_general(a, b, (((1,), (0,)), ((), ())), preferred_element_type=jnp.float32)


def dot_nt(a, b):
    return lax.dot_general(a, b, (((1,), (1,)), ((), ())), preferred_element_type=jnp.float32)


def dot_tn(a, b):
    return lax.dot_general(a, b, (((0,), (0,)), ((), ())), preferred_element_type=jnp.float32)


def swapped(v):
    lane = lax.broadcasted_iota(jnp.int32, v.shape, 1)
    return jnp.where(lane % 64 < 32, pltpu.roll(v, v.shape[1] - 32, 1), pltpu.roll(v, 32, 1))


def root(v):
    return lax.rsqrt(jnp.mean(v * v, axis=1, keepdims=True) + EPSILON)


def softmax_pair(q_pair, key, value, bias):
    outs, lses = [], []
    for h in range(2):
        q = q_pair[:, 64 * h : 64 * h + 64]
        rows, sums = [], []
        for lo, hi in ((0, 256), (256, 512)):
            s = dot_nt(q[lo:hi], key[:hi]) + bias[lo:hi, :hi]
            top = jnp.max(s, axis=1, keepdims=True)
            e = jnp.exp(s - top)
            total = jnp.sum(e, axis=1, keepdims=True)
            rows.append(dot_nn(bf16(e * (1.0 / total)), value[:hi]))
            sums.append(top + jnp.log(total))
        outs.append(jnp.concatenate(rows, axis=0))
        lses.append(jnp.concatenate(sums, axis=0))
    return jnp.concatenate(outs, axis=1), lses


def wide(ref, lo, size):
    return ref[:, :, :, :, pl.ds(lo, size)].reshape(2048, size)


def rows_of(ref, d, first=0, size=None):
    size = ref.shape[-1] if size is None else size
    return ref[d // 4, d % 4, :, :, first : first + size].reshape(256, size)


def loop(n, body, unroll=8):
    unroll = min(n, unroll)

    def several(i, carry):
        for j in range(unroll):
            body(unroll * i + j)
        return carry

    lax.fori_loop(0, n // unroll, several, 0)


def head_back(q, key, value, g, lse, bias):
    dq, dk, dv = [], None, None
    for lo, hi in ((256, 512), (0, 256)):
        s = dot_nt(q[lo:hi], key[:hi]) + bias[lo:hi, :hi]
        probs = jnp.exp(s - lse[lo:hi])
        dp = dot_nt(g[lo:hi], value[:hi])
        ds = bf16(probs * (dp - jnp.sum(probs * dp, axis=1, keepdims=True)))
        dq.insert(0, dot_nn(ds, key[:hi]))
        k_part, v_part = dot_tn(ds, q[lo:hi]), dot_tn(bf16(probs), g[lo:hi])
        if dk is None:
            dk, dv = k_part, v_part
        else:
            dk = jnp.concatenate([dk[:256] + k_part, dk[256:]], axis=0)
            dv = jnp.concatenate([dv[:256] + v_part, dv[256:]], axis=0)
    return jnp.concatenate(dq, axis=0), dk, dv


def layer_kernel(
    lengths, tokens, cot, gain_one, gain_two, query_w, key_w, value_w, out_w, gate_w, up_w, down_w,
    output, input_grad, gain_one_grad, query_grad, key_grad, value_grad, out_grad, gain_two_grad, gate_grad, up_grad,
    down_grad,
    cosine, sine, w1_own, w2_own, w3_own, w4_own, r1, r2, r3, r4, gains,
    w1, w2, w3, w4, g4, n1, bias, q_all, kv, heads, lse, part, mixed_s, mixed_grad,
    cot_all, n2_all, act, hid, d_core, d_near, d_far, dheads, act1, dk_s, dv_s, gain_in,
    b2a, b2b, b2c, b2d, b2e, b3a, b3b, b3c, b3d, b3e, b4a, b4b, b4c, b4d, b4e,
    sems, ex_s, ex_r, loc, free,
):
    p = Place()
    core, side = p.at(c=1 - p.c), p.at(zl=1 - p.zl)
    here, there = p.tensor, (1 - p.zl) * 2 + p.c
    beside, across = p.zl * 2 + 1 - p.c, (1 - p.zl) * 2 + 1 - p.c
    pair = lambda i: (sems.at[2 * i], sems.at[2 * i + 1])
    g1 = Gather(p, w1_own, w1_own, w1, *pair(0), loc.at[0])
    g2 = Gather(p, w2_own, w2_own, w2, *pair(1), loc.at[1])
    g3 = Gather(p, w3_own.at[p.zh], w3_own.at[1 - p.zh], w3, *pair(2), loc.at[2])
    gg4 = Gather(p, w4_own.at[p.zh], w4_own.at[1 - p.zh], w4, *pair(3), loc.at[3])
    cut = lambda ref, lo, size: ref.at[..., pl.ds(lo, size)]
    s1a, s1b = (
        Reduce(
            p, cut(w4, lo, size), [cut(b, lo, size) for b in (b4a, b4b, b4c, b4d, b4e)], cut(r1, lo, size),
            *pair(i), False,
        )
        for i, lo, size in ((4, 0, 256), (8, 256, 384))
    )
    s2 = Reduce(p, w2, (b2a, b2b, b2c, b2d, b2e), r2, *pair(5), False)
    s3 = Reduce(p, w3, (b3a, b3b, b3c, b3d, b3e), r3, *pair(6), True)
    s4 = Reduce(p, g4, (b4a, b4b, b4c, b4d, b4e), r4, *pair(7), True)
    ex, exp, exn, exc, exg, exo = (Pushes(ex_s.at[i], ex_r.at[i]) for i in range(6))
    cots, n2 = Column(p, cot_all, exc), Column(p, n2_all, exn)
    tok, att = d_core, n2_all

    in_cot = {k: cot_all.at[pl.ds(2 * SLOT[k], 2)] for k in LANES}
    in_part = {2: part.at[pl.ds(0, 2)], 1: part.at[pl.ds(2, 2)]}
    grads = ColumnSum(p, {**in_cot, **in_part}, d_core, d_near, d_far, exg)
    outs = ColumnSum(p, in_cot, d_core, d_near, d_far, exo)
    t = Tasks()
    got = {}

    def pack_first():
        w1_own[:, :512] = bf16(f32(query_w[...]) * scale_one)
        w1_own[:, 512:640] = bf16(jnp.concatenate([f32(key_w[...]), f32(value_w[...])], axis=1) * scale_one)

    def pack_second():
        w2_own[...] = out_w[...]

    def pack_third():
        for z in range(2):
            gate, up = (f32(w[:, 704 * z : 704 * z + 704]) * scale_two for w in (gate_w, up_w))
            w3_own[z] = bf16(jnp.concatenate([gate[:, :640], up[:, :640], gate[:, 640:], up[:, 640:]], axis=1))

    def pack_fourth():
        zero = jnp.zeros((64, 64), jnp.float32)
        for z in range(2):
            w4_own[z] = bf16(jnp.concatenate([f32(down_w[:, 704 * z : 704 * z + 704]), zero], axis=1))

    def turns():
        index = lax.broadcasted_iota(jnp.int32, (512, 128), 0)
        lane = lax.broadcasted_iota(jnp.int32, (512, 128), 1)
        freq = jnp.exp((lane % 32).astype(jnp.float32) * (-2.0 * math.log(ROPE_BASE) / HD))
        angle = (index - starts(lengths, index)).astype(jnp.float32) * freq
        cosine[...] = jnp.cos(angle)
        s = jnp.sin(angle)
        sine[...] = jnp.where(lane % 64 < 32, -s, s)

    t.add("p2", pack_second, after=("g1_N",))
    t.add("p3", pack_third, after=("p2",))
    t.add("p4", pack_fourth, after=("p3",))
    t.add("rt", turns, after=("g1_F",))
    scale_one, scale_two = column(gain_one[...]), column(gain_two[...])
    greet(everyone(p), pack_first)

    g1.steps(t, "g1", 0)
    g2.steps(t, "g2", 1, ("tok", "p2"), ("g1_O1", "g1_O-1"), ("g1_B0",), ("g1_B2",))
    g3.steps(t, "g3", 2, ("g2_Z", "p3"), ("g2_O1", "g2_O-1"), ("g2_T",), ("g2_B2",))
    gg4.steps(t, "g4", 3, ("g3_Z", "p4"), ("g3_F",), ("g3_T",), ("g3_B2",))

    def tok_push():
        tok[here] = tokens[...]
        got["z"] = ex.push(tokens, tok.at[here], side, tok.at[there])
        got["co"] = ex.push(tokens, tok.at[here], core, tok.at[beside])

    def tok_forward(ref):
        got["far"] = ex.push(ref.at[there], ref.at[there], core, ref.at[across])

    def norm(b):
        for r in range(4):
            v = f32(tok[b, 32 * r : 32 * r + 32])
            n1[pl.ds(pl.multiple_of(128 * b + 32 * r, 32), 32)] = bf16(v * root(v))

    def mask():
        for r in range(4):
            at = slice(128 * r, 128 * r + 128)
            row = lax.broadcasted_iota(jnp.int32, (128, 512), 0) + 128 * r
            col = lax.broadcasted_iota(jnp.int32, (128, 512), 1)
            bias[at] = bf16(jnp.where((col >= starts(lengths, row)) & (col <= row), 0.0, NEGATIVE))

    def cot_copy():
        cots.at(0, p.c)[...] = cot[...]

    t.add("tok", tok_push, after=("g1_Z",))
    t.add("tok_F", lambda: tok_forward(tok), lambda: [got["z"]], ("tok",))
    t.add("n_h", lambda: norm(here), after=("tok", "g1_N"))
    t.add("n_b", lambda: norm(beside), lambda: [got["co"]], ("n_h",))
    t.add("n_t", lambda: norm(there), after=("tok_F", "n_b"))
    t.add("n_a", lambda: norm(across), lambda: [got["far"]], ("n_t",))
    t.add("mk", mask, after=("g1_N",))
    t.add("c", cot_copy, after=("g1_N",))
    cots.steps(t, "c", 4, (("c", "tok_F"),) * 2)

    def project(j):
        v = dot_nn(n1[...], wide(w1, 128 * j, 128))
        r = v * cosine[...] + swapped(v) * sine[...]
        if j < 4:
            q_all[j] = bf16(r) * 0.125
        else:
            lane = lax.broadcasted_iota(jnp.int32, v.shape, 1)
            kv[...] = bf16(jnp.where(lane < 64, r, v))

    t.add("q", lambda: project(4), after=("n_a", "g1_D", "rt"))

    def attend(j):
        project(j)
        out, lses = softmax_pair(q_all[j], kv[:, :64], kv[:, 64:], bias)
        heads[:, 128 * j : 128 * j + 128] = bf16(out)
        for h in range(2):
            lse[:, 2 * j + h : 2 * j + h + 1] = lses[h]

    for j in range(4):
        t.add("a%d" % j, functools.partial(attend, j), after=("mk", "a%d" % (j - 1) if j else "q"))

    def turn():
        for b in range(4):
            at = slice(512 * b, 512 * b + 512)
            n1[:, at] = jnp.transpose(n1[:, at])

    t.add("tn", turn, after=("a3",))

    def proj():
        ex.drain()
        for d in range(8):
            part[:, :, 256 * d : 256 * d + 256] = bf16(dot_nt(heads[...], rows_of(w2, d))).reshape(4, 128, 256)
        to_core(d_far)

    def to_core(dst):
        got["ne"] = [exp.push(part.at[z * 2 + 1 - p.c], dst.at[z], core) for z in (1 - p.zl, p.zl)]

    def to_side(h, came, dst):
        at = pl.ds(64 * h, 64)
        mine = part.at[there, at]
        add_into(mine, came.at[1 - p.zl, at])
        got["z", h] = exp.push(mine, dst, side)

    def mix(h):
        for r in range(2):
            at = slice(64 * h + 32 * r, 64 * h + 32 * r + 32)
            mixed = f32(tokens[at]) + f32(part[here, at]) + f32(d_far[p.zl, at]) + f32(d_near[h, 32 * r : 32 * r + 32])
            mixed_s[at] = mixed
            n2.at(0, p.c)[at] = bf16(mixed * root(mixed))

    t.add("pj", proj, after=("a3", "g2_D"))
    for h in (0, 1):
        t.add(
            "z%d" % h, functools.partial(to_side, h, d_far, d_near.at[h]), (lambda: got["ne"][:1]) if h == 0 else None,
            ("pj",) if h == 0 else ("z0",), -5,
        )
        t.add("x%d" % h, functools.partial(mix, h), lambda h=h: [got["z", h]] + got["ne"][1 : 2 - h], ("z%d" % h,) + ("x0",) * h, -5)
    n2.steps(t, "n2", -4, (("x0",), ("x1",)))

    def gate_up(slot, n):
        at = slice(256 * slot, 256 * (slot + n))
        x_ref = n2_all.at[pl.ds(2 * slot, 2 * n)]

        def unit(gate, up):
            s = 1.0 / (1.0 + jnp.exp(-gate))
            silu = gate * s
            return silu * up, up * s * (1.0 + gate * (1.0 - s)), silu

        def body(i):
            x = x_ref[...].reshape(256 * n, 2048)
            c = pl.ds(pl.multiple_of(256 * i, 256), 256)
            e = pl.ds(pl.multiple_of(640 + 256 * i, 128), 256)
            h, a, b = unit(dot_nn(x, wide(w3, c.start, 256)), dot_nn(x, wide(w3, e.start, 256)))
            hid[at, c] = bf16(h)
            act[at, c] = bf16(a)
            act[at, e] = bf16(b)

        loop(2, body)
        x = x_ref[...].reshape(256 * n, 2048)
        v = dot_nn(x, wide(w3, 1152, 256))
        h, a, b = unit(dot_nn(x, wide(w3, 512, 128)), v[:, :128])
        hid[at, 512:640] = bf16(h)
        act[at, 512:640] = bf16(a)
        act[at, 1152:1280] = bf16(b)
        v = v[:, 128:]
        h, a, b = unit(v, pltpu.roll(v, 64, 1))
        lane = lax.broadcasted_iota(jnp.int32, v.shape, 1)
        hid[at, 640:768] = bf16(jnp.where(lane < 64, h, 0.0))
        act[at, 1280:1408] = bf16(jnp.where(lane < 64, a, pltpu.roll(b, 64, 1)))

    ups = ("gu0", "gu1", "gu2")
    for name, slot, n, blocks in (("gu0", 3, 1, (0,)), ("gu1", 1, 2, (1, -1)), ("gu2", 0, 1, (2,))):
        t.add(name, functools.partial(gate_up, slot, n), after=("g3_D",) + tuple("n2_C%d" % k for k in blocks))

    def deep4(d):
        c = pl.ds(pl.multiple_of(256 * d, 256), 256)
        x = cot_all[:, :, c].reshape(1024, 256)
        g4[d // 4, d % 4] = bf16(dot_tn(x, hid[...])).reshape(4, 64, 768)

    cot_here = tuple("c_C%d" % k for k in ORDER)
    t.add("dw4", lambda: loop(8, deep4), after=ups + cot_here)
    s4.steps(t, "re", 1, ("dw4",))

    def hidden_grad(slot, n):
        at = slice(256 * slot, 256 * (slot + n))
        x = cot_all[2 * slot : 2 * (slot + n)].reshape(256 * n, 2048)
        for i in range(2):
            g = dot_nn(x, wide(w4, 256 * i, 256))
            for lo in (256 * i, 640 + 256 * i):
                act[at, lo : lo + 256] = bf16(g * f32(act[at, lo : lo + 256]))
        g = dot_nn(x, wide(w4, 512, 256))
        for lo in (512, 1152):
            act[at, lo : lo + 128] = bf16(g[:, :128] * f32(act[at, lo : lo + 128]))
        g = g[:, 128:]
        act[at, 1280:1408] = bf16((g + pltpu.roll(g, 64, 1)) * f32(act[at, 1280:1408]))

    t.add("hg1", lambda: hidden_grad(1, 3), after=("g4_D", "gu0", "gu1", "c_C1", "c_C-1", "c_C0"))
    t.add("hg2", lambda: hidden_grad(0, 1), after=("g4_D", "gu2", "c_C2"))

    def back(slot, dst):
        at = slice(256 * slot, 256 * slot + 512)

        def deep(d):
            c = pl.ds(pl.multiple_of(256 * d, 256), 256)
            dst[:, :, c] = bf16(dot_nt(act[at], rows_of(w3, d))).reshape(4, 128, 256)

        loop(8, deep)

    def back_far():
        exp.drain()
        back(0, part)
        grads.ready(2)
        grads.ready(1)

    def back_near():
        exc.drain()
        back(2, cot_all.at[pl.ds(4, 4)])
        grads.ready(-1)
        grads.ready(0)

    t.add("k2", back_far, after=("hg1", "hg2"))
    t.add("k0", back_near, after=("dw4", "hg1", "hg2"))
    grads.steps(t, "gr", -4, {2: "k2", 1: "k2", -1: "k0"}, ("n2_C1", "n2_C-1"))

    def deep3(d):
        c = pl.ds(pl.multiple_of(256 * d, 256), 256)
        x = n2_all[:, :, c].reshape(1024, 256)
        w3[d // 4, d % 4] = bf16(dot_tn(x, act[...])).reshape(4, 64, 1408)

    def dw3():
        g3.drain()
        loop(8, deep3)
        exn.drain()
        for device in (core, side):
            pl.semaphore_signal(free.at[2], inc=1, device_id=device, device_id_type=MESH)

    t.add("dw3", dw3, after=("k2", "k0"))
    s3.steps(t, "rd", 2, ("dw3",))

    def mixed_back():
        for r in range(4):
            at = slice(32 * r, 32 * r + 32)
            mixed = mixed_s[at]
            factor = root(mixed)
            unit = mixed * factor
            grad = grads.total(at)
            v = f32(cot[at]) + factor * (grad - unit * jnp.mean(grad * unit, axis=1, keepdims=True))
            mixed_grad[at] = v
            att[here, at] = bf16(v)
        for device in (core, p.at_z(1), p.at_z(-1)):
            pl.semaphore_signal(free.at[0], inc=1, device_id=device, device_id_type=MESH)
        exg.drain()
        pl.semaphore_wait(free.at[2], 2)
        for h in (0, 1):
            at = pl.ds(64 * h, 64)
            got["z", h] = ex.push(att.at[here, at], att.at[here, at], side, att.at[there, at])
        got["co"] = ex.push(att.at[here], att.at[here], core, att.at[beside])

    def att_forward(h):
        at = pl.ds(64 * h, 64)
        got["far", h] = ex.push(att.at[there, at], att.at[there, at], core, att.at[across, at])

    t.add("mb", mixed_back, grads.arrived, ("k0", "gr_A1", "gr_A-1", "dw3"), -6)
    t.add("att0", lambda: att_forward(0), lambda: [got["z", 0]], ("mb",), -6)
    t.add("att", lambda: att_forward(1), lambda: [got["z", 1]], ("att0",), -6)

    def out_rows(d):
        c = pl.ds(pl.multiple_of(256 * d, 256), 256)
        for i in range(2):
            o = dot_nt(hid[512 * i : 512 * i + 512], rows_of(w4, d))
            cot_all[4 * i : 4 * i + 4, :, c] = bf16(o).reshape(4, 128, 256)

    def out_send():
        pl.semaphore_wait(free.at[0], 3)
        for k in LANES:
            outs.ready(k)

    def out_end():
        for r in range(4):
            at = slice(32 * r, 32 * r + 32)
            output[at] = bf16(mixed_s[at] + outs.total(at))

    t.add("o", lambda: loop(8, out_rows), after=("mb",), rank=6)
    t.add("o_S", out_send, after=("o", "att"), rank=6)
    outs.steps(t, "ou", 6, {k: "o_S" for k in LANES})
    t.add("o_D", out_end, outs.arrived, ("ou_A1", "ou_A-1"), 7)

    def heads_back():
        for j in range(2):
            dheads[:, 256 * j : 256 * j + 256] = bf16(dot_nn(att[0:4].reshape(512, 2048), wide(w2, 256 * j, 256)))

    def deep2(d):
        c = pl.ds(pl.multiple_of(256 * d, 256), 256)
        w2[d // 4, d % 4] = bf16(dot_tn(att[0:4, :, c].reshape(512, 256), heads[...])).reshape(4, 64, 512)

    def dw2():
        g2.drain()
        loop(8, deep2)

    t.add("h", heads_back, lambda: [got["co"], got["far", 0], got["far", 1]], ("att",))
    t.add("dw2", dw2, after=("h",))
    s2.steps(t, "rc", 3, ("dw2",))

    def attend_back(j):
        key, value = kv[:, :64], kv[:, 64:]
        dqs = []
        for h in range(2):
            at = slice(128 * j + 64 * h, 128 * j + 64 * h + 64)
            dq, dk, dv = head_back(
                q_all[j, :, 64 * h : 64 * h + 64], key, value, dheads[:, at], lse[:, 2 * j + h : 2 * j + h + 1], bias
            )
            dqs.append(dq)
            if j + h == 0:
                dk_s[...] = dk
                dv_s[...] = dv
            else:
                dk_s[...] += dk
                dv_s[...] += dv
        v = jnp.concatenate(dqs, axis=1) * 0.125
        act1[:, 128 * j : 128 * j + 128] = bf16(v * cosine[...] - swapped(v) * sine[...])
        if j == 3:
            v = jnp.concatenate([dk_s[...], dv_s[...]], axis=1)
            lane = lax.broadcasted_iota(jnp.int32, v.shape, 1)
            act1[:, 512:640] = bf16(jnp.where(lane < 64, v * cosine[...] - swapped(v) * sine[...], v))

    for j in range(4):
        t.add("ab%d" % j, functools.partial(attend_back, j), after=("ab%d" % (j - 1) if j else "h",))

    def deep(d):
        c = pl.ds(pl.multiple_of(256 * d, 256), 256)
        part[:, :, c] = bf16(dot_nt(act1[...], rows_of(w1, d))).reshape(4, 128, 256)

    def deep1(lo, size, d):
        x = n1[pl.ds(pl.multiple_of(256 * (d % 2), 256), 256), pl.ds(pl.multiple_of(512 * (d // 2), 512), 512)]
        w4[d // 4, d % 4, :, :, lo : lo + size] = bf16(dot_nn(x, act1[:, lo : lo + size])).reshape(4, 64, size)

    def project_back():
        loop(8, deep)
        to_core(att.at[pl.ds(4, 2)])

    def dw1a():
        gg4.drain()
        loop(8, functools.partial(deep1, 0, 256))
        pl.semaphore_wait(free.at[1], 5)

    def s4_end():
        s4.finish()
        for device in [p.partner()] + [p.ring(a, k) for a in "xy" for k in WAYS]:
            pl.semaphore_signal(free.at[1], inc=1, device_id=device, device_id_type=MESH)

    def last(h):
        for r in range(2):
            at = slice(64 * h + 32 * r, 64 * h + 32 * r + 32)
            v = f32(tokens[at])
            factor = root(v)
            unit = v * factor
            grad = f32(part[here, at]) + f32(att[4 + p.zl, at]) + f32(att[6, at])
            input_grad[at] = bf16(
                mixed_grad[at] + factor * (grad - unit * jnp.mean(grad * unit, axis=1, keepdims=True))
            )

    _, need, after, _ = t.all["re_D"]
    t.add("re_D", s4_end, need, after, 1)
    t.add("dn1", project_back, after=("ab3",))
    t.add("da", dw1a, after=("ab1", "re_D", "o", "tn"))
    t.add("db", lambda: loop(8, functools.partial(deep1, 256, 384)), after=("ab3", "da"))
    for h in (0, 1):
        t.add(
            "w%d" % h, functools.partial(to_side, h, att.at[pl.ds(4, 2)], att.at[6, pl.ds(64 * h, 64)]),
            (lambda: got["ne"][:1]) if h == 0 else None, ("dn1",) if h == 0 else ("w0",), -5,
        )
        t.add("l%d" % h, functools.partial(last, h), lambda h=h: [got["z", h]] + got["ne"][1 : 2 - h], ("w%d" % h,) + ("last0",) * h, 8)
    s1a.steps(t, "ra", 4, ("da",))
    s1b.steps(t, "rb", 5, ("db",))

    def gain_sum(own, grad):
        return jnp.sum(f32(own) * grad, axis=1, keepdims=True)

    def gain_two_sum():
        gains[...] = jnp.broadcast_to(gain_sum(w3_own[0], r3[0]) + gain_sum(w3_own[1], r3[1]), (64, 128))

    def gain_one_sum():
        lane = lax.broadcasted_iota(jnp.int32, (64, 128), 1)
        gain_in[here] = jnp.where(lane == 0, gain_sum(w1_own[...], r1[...]), gains[...])
        got["y"] = [
            ex.push(gain_in.at[here], gain_in.at[here], device, gain_in.at[at])
            for device, at in ((core, beside), (side, there), (p.at(zl=1 - p.zl, c=1 - p.c), across))
        ]

    def gain_end():
        total = (gain_in[0] + gain_in[1]) + (gain_in[2] + gain_in[3])
        gain_one_grad[...] = row(total[:, 0:1] / scale_one)
        gain_two_grad[...] = row(total[:, 1:2] / scale_two)

    def first_end():
        query_grad[...] = r1[:, :512] * scale_one
        v = r1[:, 512:640] * scale_one
        key_grad[...] = v[:, :64]
        value_grad[...] = v[:, 64:]

    def second_end():
        out_grad[...] = r2[...]

    def third_end():
        for ref, lo, tail in ((gate_grad, 0, 1280), (up_grad, 640, 1344)):
            pieces = [v for z in range(2) for v in (r3[z, :, lo : lo + 640], r3[z, :, tail : tail + 64])]
            ref[...] = jnp.concatenate(pieces, axis=1) * scale_two

    def fourth_end():
        down_grad[...] = jnp.concatenate([r4[0, :, :704], r4[1, :, :704]], axis=1)

    t.add("y2", gain_two_sum, after=("rd_D",), rank=40)
    t.add("y1", gain_one_sum, after=("y2", "ra_D", "rb_D"), rank=40)
    t.add("y", gain_end, lambda: got["y"], ("y1",), 50)
    for i, (end, after) in enumerate(
        ((first_end, ("y1",)), (second_end, ("rc_D",)), (third_end, ("rd_D",)), (fourth_end, ("re_D",)))
    ):
        t.add("e%d" % i, end, after=after, rank=45)
    t.run(PLAN)
    for group in (g1, s1a, s1b, s2, s3, s4, ex, exp, exo):
        group.drain()


def layer(*args):
    vmem = pl.BlockSpec(memory_space=pltpu.VMEM)
    full = lambda *s: jax.ShapeDtypeStruct(s, jnp.float32)
    half = lambda *s: jax.ShapeDtypeStruct(s, jnp.bfloat16)
    dma, held, wide32 = pltpu.SemaphoreType.DMA, lambda *s: pltpu.VMEM(s, jnp.bfloat16), lambda *s: pltpu.VMEM(s, jnp.float32)
    weight = lambda c: held(2, 4, 4, 64, c)
    return pl.pallas_call(
        layer_kernel,
        out_shape=[
            half(128, 2048), half(128, 2048), full(1, 64),
            full(64, 512), full(64, 64), full(64, 64), full(64, 512),
            full(1, 64), full(64, 1408), full(64, 1408), full(64, 1408),
        ],
        in_specs=[pl.BlockSpec(memory_space=pltpu.SMEM)] + [vmem] * 11,
        out_specs=[vmem] * 11,
        scratch_shapes=[
            wide32(512, 128), wide32(512, 128),
            held(64, 640), held(64, 512), held(2, 64, 1408), held(2, 64, 768),
            wide32(64, 640), wide32(64, 512), wide32(2, 64, 1408), wide32(2, 64, 768), wide32(64, 128),
            weight(640), weight(512), weight(1408), weight(768), weight(768),
            held(512, 2048), held(512, 512), held(4, 512, 128), held(512, 128), held(512, 512),
            wide32(512, 8), held(4, 128, 2048),
            wide32(128, 2048), wide32(128, 2048),
            held(8, 128, 2048), held(8, 128, 2048), held(1024, 1408), held(1024, 768),
            held(4, 128, 2048), held(2, 64, 2048), held(2, 128, 2048),
            held(512, 512), held(512, 640), wide32(512, 64), wide32(512, 64), wide32(4, 64, 128),
        ]
        + reduce_buffers(512) + reduce_buffers(1408) + reduce_buffers(768)
        + [dma((18, 64)), dma((6, 24)), dma((6, 24)), dma((4,)), pltpu.SemaphoreType.REGULAR((3,))],
        compiler_params=pltpu.CompilerParams(collective_id=0, has_side_effects=True, vmem_limit_bytes=62 * 2**20),
    )(*args)


def hand_on_kernel(*refs):
    n = len(refs) // 2
    sems = refs[-1]
    copies = [pltpu.make_async_copy(refs[i], refs[n + i], sems.at[i]) for i in range(n)]
    for copy in copies:
        copy.start()
    for copy in copies:
        copy.wait()


def hand_on(arrays):
    n = len(arrays)
    return pl.pallas_call(
        hand_on_kernel,
        out_shape=[jax.ShapeDtypeStruct(v.shape, v.dtype) for v in arrays],
        in_specs=[pl.BlockSpec(memory_space=pl.ANY)] * n,
        out_specs=[pl.BlockSpec(memory_space=pltpu.VMEM)] * n,
        scratch_shapes=[pltpu.SemaphoreType.DMA((n,))],
        compiler_params=pltpu.CompilerParams(vmem_limit_bytes=62 * 2**20),
    )(*arrays)


def shards(
    tokens,
    lengths,
    attention_gain,
    query_weight,
    key_weight,
    value_weight,
    out_weight,
    feedforward_gain,
    gate_weight,
    up_weight,
    down_weight,
    cotangent,
):
    outs = layer(
        lengths, tokens, cotangent, attention_gain[None], feedforward_gain[None], query_weight, key_weight, value_weight,
        out_weight.T, gate_weight, up_weight, down_weight.T,
    )
    outs = hand_on(outs)
    turned = (6, 10)
    return tuple(v.T if i in turned else v[0] if v.shape[0] == 1 else v for i, v in enumerate(outs))


def solution(mesh):
    return jax.shard_map(
        shards,
        mesh=mesh,
        in_specs=(
            P(("dp", "tensor"), None),
            P("dp", None),
            P("dp"),
            P("dp", "tensor"),
            P("dp", "tensor"),
            P("dp", "tensor"),
            P("tensor", "dp"),
            P("dp"),
            P("dp", "tensor"),
            P("dp", "tensor"),
            P("tensor", "dp"),
            P(("dp", "tensor"), None),
        ),
        out_specs=(
            P(("dp", "tensor"), None),
            P(("dp", "tensor"), None),
            P("dp"),
            P("dp", "tensor"),
            P("dp", "tensor"),
            P("dp", "tensor"),
            P("tensor", "dp"),
            P("dp"),
            P("dp", "tensor"),
            P("dp", "tensor"),
            P("tensor", "dp"),
        ),
        check_vma=False,
    )
```
